128 devices in a mesh: tower: 2 (over z_hi), seq: 8 (over x, core), rep: 8 (over y, z_lo).
Axes of the slice: x: 4, y: 4, z: 4 (z_hi: 2, z_lo: 2; z = z_hi * 2 + z_lo), core: 2. Of those that a mesh axis runs over, the one named last changes fastest.
Arguments:
- queries: bfloat16 [2, 3072, 3072], P('tower', 'seq', 'rep'), may hold values from -8.1 to 8.1
- key_input: bfloat16 [2, 3072, 3072], P('tower', 'seq', 'rep'), may hold values from -8.1 to 8.1
- values: bfloat16 [2, 3072, 3072], P('tower', 'seq', 'rep'), may hold values from -6 to 6
- cotangent: bfloat16 [2, 3072, 3072], P('tower', 'seq', 'rep'), may hold values from -6 to 6
- positions: int32 [2, 3072], P('tower', 'seq'), may hold values from 0 to 1023
- lengths: int32 [2, 8], P('tower', 'seq'), may hold values from 2 to 384, as said below
Outputs:
- attended: bfloat16 [2, 3072, 3072], P('tower', 'seq', 'rep')
- grad_query: bfloat16 [2, 3072, 3072], P('tower', 'seq', 'rep')
- grad_key: bfloat16 [2, 3072, 3072], P('tower', 'seq', 'rep')
- grad_value: bfloat16 [2, 3072, 3072], P('tower', 'seq', 'rep')
The draws below stay inside these ranges and needn't reach their ends.
Inputs may be any that keep to these rules, and one draw needn't show every extreme that they name: In each block of 384 slots the first lengths slots hold tokens and the rest are padding.
All inputs are finite; a program needn't handle non-finite values.
Results may differ from the reference program's by a relative error of at most 0.012.
The reference program's roundings to bfloat16 on the way count: a program that leaves them out, or rounds other values in their place, can miss the bound.
Values may be sent and summed in bfloat16 or wider, within the bound.
A program may use at most 128 MiB of HBM per device.

```python
import math
import jax
import jax.numpy as jnp
from jax import lax

HEADS = 24
HEAD_DIM = 128
TOK_DEV = 384
SPAN = 1024
SEQ = 3072


def planted(key):
    helper_key = jax.random.fold_in(key, 101)
    shard_total = SEQ // TOK_DEV
    chosen = jax.random.randint(jax.random.fold_in(helper_key, 1), (shard_total,), 0, 4) == 0
    chosen = chosen.at[0].set(True)
    anchor = jax.random.randint(jax.random.fold_in(helper_key, 4), (shard_total,), 0, SPAN)
    return (chosen, anchor)


def draw_queries(key, part):
    key = jax.random.fold_in(key, 7)
    array_shape = (2, SEQ // TOK_DEV, TOK_DEV, HEADS * HEAD_DIM)
    drawn = jnp.clip(jax.random.normal(key, array_shape, jnp.float32), -4.0, 4.0)
    return drawn.reshape(2, SEQ, HEADS * HEAD_DIM).astype(jnp.bfloat16)


def draw_key_input(key, part):
    key = jax.random.fold_in(key, 9)
    array_shape = (2, SEQ // TOK_DEV, TOK_DEV, HEADS * HEAD_DIM)
    drawn = jnp.clip(jax.random.normal(key, array_shape, jnp.float32), -4.0, 4.0)
    return drawn.reshape(2, SEQ, HEADS * HEAD_DIM).astype(jnp.bfloat16)


def draw_positions(key, part):
    chosen, anchor = planted(key)
    key = jax.random.fold_in(key, 13)
    drawn = jax.random.randint(key, (2, SEQ // TOK_DEV, TOK_DEV), 0, SPAN)
    tied = jnp.where(chosen[None, :], anchor[None, :], drawn[:, :, 0])
    drawn = drawn.at[:, :, 0].set(tied).at[:, :, 1].set(tied)
    return drawn.reshape(2, SEQ).astype(jnp.int32)


def draw_lengths(key, part):
    key = jax.random.fold_in(key, 17)
    shard_total = SEQ // TOK_DEV
    video = jax.random.randint(jax.random.fold_in(key, 1), (shard_total,), TOK_DEV // 2, TOK_DEV + 1)
    video = video.at[0].set(TOK_DEV)
    audio = jax.random.randint(jax.random.fold_in(key, 2), (shard_total,), TOK_DEV // 3, TOK_DEV + 1)
    audio = audio.at[shard_total - 1].set(2)
    return jnp.stack([video, audio]).astype(jnp.int32)


def block_scale(stream_key, dims, cuts, smallest, high):
    level, own = 1.0, jax.random.fold_in(stream_key, 6)
    for position, shards_of in cuts:
        steps = jnp.exp(jax.random.uniform(jax.random.fold_in(own, position), (shards_of,), jnp.float32, smallest / len(cuts), high / len(cuts)))
        level = level * jnp.repeat(steps, dims[position] // shards_of).reshape([-1 if axis == position else 1 for axis in range(len(dims))])
    return level


def centred(stream_key, shape, spread, reach, pieces=(), kind=jnp.bfloat16):
    level = block_scale(stream_key, shape, pieces, -0.22, 0.18) if pieces else 1.0
    values = jax.random.normal(stream_key, shape, jnp.float32) * spread * level
    return jnp.minimum(jnp.maximum(values, -reach), reach).astype(kind)


def setup_inputs(seed: int = 0) -> dict:
    arg_keys = jax.random.split(jax.random.key(seed), 7)
    queries = draw_queries(jax.random.fold_in(arg_keys[6], 71), 0)
    key_input = draw_key_input(jax.random.fold_in(arg_keys[6], 71), 0)
    values = centred(arg_keys[2], (2, SEQ, HEADS * HEAD_DIM), 1.0, 6.0, ((0, 2), (1, 8), (2, 8)))
    cotangent = centred(arg_keys[3], (2, SEQ, HEADS * HEAD_DIM), 1.0, 6.0, ((0, 2), (1, 8), (2, 8)))
    positions = draw_positions(jax.random.fold_in(arg_keys[6], 71), 0)
    lengths = draw_lengths(jax.random.fold_in(arg_keys[6], 71), 0)
    return {"queries": queries, "key_input": key_input, "values": values, "cotangent": cotangent, "positions": positions, "lengths": lengths}


def phases(positions, width):
    half_width = width // 2
    rates = jnp.exp(-math.log(10000.0) * jnp.arange(half_width, dtype=jnp.float32) / half_width)
    angles = positions.astype(jnp.float32)[..., None] * rates
    return (jnp.cos(angles)[..., None, :], jnp.sin(angles)[..., None, :])

def rotate(tensor, cosine_table, sine_table):
    half_width = tensor.shape[-1] // 2
    leading = tensor[..., :half_width]
    trailing = tensor[..., half_width:]
    return jnp.concatenate([leading * cosine_table - trailing * sine_table, trailing * cosine_table + leading * sine_table], axis=-1)

def unrotate(tensor, cosine_table, sine_table):
    half_width = tensor.shape[-1] // 2
    leading = tensor[..., :half_width]
    trailing = tensor[..., half_width:]
    return jnp.concatenate([leading * cosine_table + trailing * sine_table, trailing * cosine_table - leading * sine_table], axis=-1)

def branch(query_rows, grad_rows, key_rows, value_rows, key_valid, scaling):
    scores = jnp.dot(query_rows, key_rows.T, preferred_element_type=jnp.float32) * scaling
    scores = jnp.where(key_valid[None, :], scores, -jnp.inf)
    largest = lax.optimization_barrier(jnp.max(scores, axis=1, keepdims=True))
    log_total = largest + jnp.log(lax.optimization_barrier(jnp.sum(jnp.exp(scores - largest), axis=1, keepdims=True)))
    probabilities = jnp.exp(scores - log_total).astype(jnp.bfloat16)
    branch_out = jnp.dot(probabilities, value_rows, preferred_element_type=jnp.float32)
    row_dot = lax.optimization_barrier(jnp.sum(grad_rows.astype(jnp.float32) * branch_out, axis=1, keepdims=True))
    value_grad = jnp.dot(probabilities.T, grad_rows, preferred_element_type=jnp.float32)
    prob_grad = jnp.dot(grad_rows, value_rows.T, preferred_element_type=jnp.float32)
    score_grad = (probabilities.astype(jnp.float32) * (prob_grad - row_dot) * scaling).astype(jnp.bfloat16)
    query_grad = jnp.dot(score_grad, key_rows, preferred_element_type=jnp.float32)
    key_grad = jnp.dot(score_grad.T, query_rows, preferred_element_type=jnp.float32)
    return (branch_out, query_grad, key_grad, value_grad)

def reference(queries, key_input, values, cotangent, positions, lengths):
    slot_index = jnp.arange(SEQ, dtype=jnp.int32) % TOK_DEV
    is_valid = slot_index[None, :] < jnp.repeat(lengths, TOK_DEV, axis=1)
    cosine_table, sine_table = phases(positions, HEAD_DIM)
    shaped = (2, SEQ, HEADS, HEAD_DIM)
    rot_queries = rotate(queries.reshape(shaped).astype(jnp.float32), cosine_table, sine_table).astype(jnp.bfloat16)
    rot_keys = rotate(key_input.reshape(shaped).astype(jnp.float32), cosine_table, sine_table).astype(jnp.bfloat16)
    value_heads = values.reshape(shaped)
    grad_heads = jnp.where(is_valid[:, :, None, None], cotangent.reshape(shaped), jnp.zeros((), jnp.bfloat16))
    scaling = 1.0 / math.sqrt(HEAD_DIM)

    def select_head(array, head_index):
        return lax.dynamic_index_in_dim(array, head_index, 2, keepdims=False)

    def one_head(head_index):
        query_rows = select_head(rot_queries, head_index)
        key_rows = select_head(rot_keys, head_index)
        value_rows = select_head(value_heads, head_index)
        grad_rows = select_head(grad_heads, head_index)
        out_list = []
        qgrad_list = []
        kgrad_sum = [jnp.zeros((SEQ, HEAD_DIM), jnp.float32), jnp.zeros((SEQ, HEAD_DIM), jnp.float32)]
        vgrad_sum = [jnp.zeros((SEQ, HEAD_DIM), jnp.float32), jnp.zeros((SEQ, HEAD_DIM), jnp.float32)]
        for query_side in range(2):
            out_total = jnp.zeros((SEQ, HEAD_DIM), jnp.float32)
            qgrad_total = jnp.zeros((SEQ, HEAD_DIM), jnp.float32)
            for key_side in range(2):
                branch_out, query_grad, key_grad, value_grad = branch(query_rows[query_side], grad_rows[query_side], key_rows[key_side], value_rows[key_side], is_valid[key_side], scaling)
                out_total = out_total + branch_out
                qgrad_total = qgrad_total + query_grad
                kgrad_sum[key_side] = kgrad_sum[key_side] + key_grad
                vgrad_sum[key_side] = vgrad_sum[key_side] + value_grad
            out_list.append(out_total.astype(jnp.bfloat16))
            qgrad_list.append(qgrad_total.astype(jnp.bfloat16))
        return (jnp.stack(out_list), jnp.stack(qgrad_list), jnp.stack(kgrad_sum).astype(jnp.bfloat16), jnp.stack(vgrad_sum).astype(jnp.bfloat16))
    head_outs, head_qgrads, head_kgrads, head_vgrads = lax.map(one_head, jnp.arange(HEADS, dtype=jnp.int32))
    merged_out = jnp.moveaxis(head_outs, 0, 2)
    merged_qgrad = lax.optimization_barrier(jnp.moveaxis(head_qgrads, 0, 2))
    merged_kgrad = lax.optimization_barrier(jnp.moveaxis(head_kgrads, 0, 2))
    merged_vgrad = jnp.moveaxis(head_vgrads, 0, 2)
    attended = jnp.where(is_valid[:, :, None, None], merged_out, jnp.zeros((), jnp.bfloat16))
    grad_query = unrotate(merged_qgrad.astype(jnp.float32), cosine_table, sine_table).astype(jnp.bfloat16)
    grad_key = unrotate(merged_kgrad.astype(jnp.float32), cosine_table, sine_table).astype(jnp.bfloat16)
    full_width = HEADS * HEAD_DIM
    return (attended.reshape(2, SEQ, full_width), grad_query.reshape(2, SEQ, full_width), grad_key.reshape(2, SEQ, full_width), merged_vgrad.reshape(2, SEQ, full_width))
```

```python
import math

import jax
import jax.numpy as jnp
import numpy as np
from jax import lax
from jax.experimental import pallas as pl
from jax.experimental.pallas import tpu as pltpu
from jax.sharding import PartitionSpec as P

HEAD_DIM = 128
HEADS_DEV = 3
TOK = 384
ROWS = 4 * TOK
HALF = 2 * TOK
SCALE = 1.0 / math.sqrt(HEAD_DIM)
SCALE_LOG2 = SCALE * math.log2(math.e)
MESH = pl.DeviceIdType.MESH
NN = (((1,), (0,)), ((), ()))
NT = (((1,), (1,)), ((), ()))
f32 = jnp.float32
bf16 = jnp.bfloat16

(
    K_R, K_L, V_R, V_L, K_FWD, V_FWD,
    Q_S, Q_T, Q_FWD, G_S, G_T, G_FWD,
    STATS, O_S1, O_S3, O_T, DQ_S1, DQ_S3, DQ_T,
    DK3, DV3, DV2, DK1, DK2, DV1,
    LEN_R, LEN_L, LEN_FWD,
) = range(28)


def dot(a, b, dims):
    return lax.dot_general(a, b, dims, preferred_element_type=f32)


def kernel(
    q_in, k_in, v_in, g_in, pos_in, len_in, rate_in,
    o_out, dq_out, dk_out, dv_out,
    kbuf, vbuf, ktbuf, vtbuf, qt, gt, lens,
    score, prob, dscore, gts,
    stat_out, stat_in, oq_own, oq_send, oq_recv,
    kv_own, kv_send, kv_recv, tables,
    send_sem, recv_sem,
):
    t, s, r = lax.axis_index("tower"), lax.axis_index("seq"), lax.axis_index("rep")
    right = (t, lax.rem(s + 2, 8), r)
    left = (t, lax.rem(s + 6, 8), r)
    sibling = (t, s + 1 - 2 * lax.rem(s, 2), r)
    peer = (1 - t, s, r)

    def copy(kind, h, src, dst, target):
        return pltpu.make_async_remote_copy(
            src_ref=src, dst_ref=dst,
            send_sem=send_sem.at[kind, h], recv_sem=recv_sem.at[kind, h],
            device_id=target, device_id_type=MESH,
        )

    def rows(slot):
        return pl.ds(slot * TOK, TOK)

    def describe(kind, h):
        own, first, second, third = rows(0), rows(1), rows(2), rows(3)
        cols = pl.ds(h * HEAD_DIM, HEAD_DIM)
        table = {
            K_R: lambda: (kbuf.at[h, own], kbuf.at[h, first], right),
            K_L: lambda: (kbuf.at[h, own], kbuf.at[h, second], left),
            V_R: lambda: (vbuf.at[h, own], vbuf.at[h, first], right),
            V_L: lambda: (vbuf.at[h, own], vbuf.at[h, second], left),
            K_FWD: lambda: (kbuf.at[h, first], kbuf.at[h, third], right),
            V_FWD: lambda: (vbuf.at[h, second], vbuf.at[h, third], left),
            Q_S: lambda: (qt.at[h, :, own], qt.at[h, :, first], sibling),
            Q_T: lambda: (qt.at[h, :, own], qt.at[h, :, second], peer),
            Q_FWD: lambda: (qt.at[h, :, second], qt.at[h, :, third], sibling),
            G_S: lambda: (gt.at[h, :, own], gt.at[h, :, first], sibling),
            G_T: lambda: (gt.at[h, :, own], gt.at[h, :, second], peer),
            G_FWD: lambda: (gt.at[h, :, second], gt.at[h, :, third], sibling),
            STATS: lambda: (stat_out.at[h], stat_in.at[h], sibling),
            O_S1: lambda: (oq_send.at[h, 0, 0], oq_recv.at[h, 0, 0], sibling),
            O_S3: lambda: (oq_send.at[h, 0, 1], oq_recv.at[h, 0, 1], sibling),
            O_T: lambda: (oq_send.at[h, 0, 2], oq_recv.at[h, 0, 2], peer),
            DQ_S1: lambda: (oq_send.at[h, 1, 0], oq_recv.at[h, 1, 0], sibling),
            DQ_S3: lambda: (oq_send.at[h, 1, 1], oq_recv.at[h, 1, 1], sibling),
            DQ_T: lambda: (oq_send.at[h, 1, 2], oq_recv.at[h, 1, 2], peer),
            DK3: lambda: (kv_send.at[h, 0], kv_recv.at[h, 0], right),
            DV3: lambda: (kv_send.at[h, 1], kv_recv.at[h, 1], left),
            DV2: lambda: (kv_send.at[h, 2], kv_recv.at[h, 2], right),
            DK1: lambda: (kv_send.at[h, 3], kv_recv.at[h, 3], left),
            DK2: lambda: (kv_send.at[h, 4], kv_recv.at[h, 4], right),
            DV1: lambda: (kv_send.at[h, 5], kv_recv.at[h, 5], left),
            LEN_R: lambda: (lens.at[0], lens.at[1], right),
            LEN_L: lambda: (lens.at[0], lens.at[2], left),
            LEN_FWD: lambda: (lens.at[1], lens.at[3], right),
        }
        return copy(kind, h, *table[kind]())

    def start(kind, h):
        describe(kind, h).start()

    def arrived(kind, h):
        describe(kind, h).wait_recv()

    barrier = pltpu.get_barrier_semaphore()
    for device in (right, left, sibling, peer):
        pl.semaphore_signal(barrier, inc=1, device_id=device, device_id_type=MESH)

    length = len_in[...]
    lens[0] = jnp.broadcast_to(length, (8, 128))
    for h in range(HEADS_DEV):
        vbuf[h, 0:TOK, :] = v_in[0, :, h * HEAD_DIM : (h + 1) * HEAD_DIM]

    pl.semaphore_wait(barrier, 4)
    start(V_R, 0)
    start(V_L, 0)
    start(LEN_R, 0)
    start(LEN_L, 0)

    angles = rate_in[:, 0:1] * pos_in[...].astype(f32)
    cos, sin = jnp.cos(angles), jnp.sin(angles)
    tables[0:64, :] = cos
    tables[64:128, :] = sin
    turned = jnp.transpose(tables[...])
    swapped = pltpu.roll(turned, 64, 1)
    low = lax.broadcasted_iota(jnp.int32, (TOK, HEAD_DIM), 1) < 64
    cos_rows = jnp.where(low, turned, swapped)
    sin_rows = jnp.where(low, -swapped, turned)
    present_rows = lax.broadcasted_iota(jnp.int32, (TOK, HEAD_DIM), 0) < length
    present_cols = lax.broadcasted_iota(jnp.int32, (1, TOK), 1) < length

    def prepare_keys(h):
        key = k_in[0, :, h * HEAD_DIM : (h + 1) * HEAD_DIM].astype(f32)
        key = key * cos_rows + pltpu.roll(key, 64, 1) * sin_rows
        key = jnp.where(present_rows, key, key[0:1, :])
        kbuf[h, 0:TOK, :] = key.astype(bf16)

    def prepare_queries(h):
        cols = slice(h * HEAD_DIM, (h + 1) * HEAD_DIM)
        query = jnp.transpose(q_in[0, :, cols].astype(f32))
        x1, x2 = query[0:64, :], query[64:128, :]
        qt[h, 0:64, 0:TOK] = (x1 * cos - x2 * sin).astype(bf16)
        qt[h, 64:128, 0:TOK] = (x2 * cos + x1 * sin).astype(bf16)
        grad = jnp.transpose(g_in[0, :, cols].astype(f32))
        gt[h, :, 0:TOK] = jnp.where(present_cols, grad, 0.0).astype(bf16)

    def send_keys(h):
        start(K_R, h)
        start(K_L, h)

    def send_values(h):
        start(V_R, h)
        start(V_L, h)

    def send_queries(h):
        start(Q_T, h)
        start(Q_S, h)
        start(G_T, h)
        start(G_S, h)

    def forward_keys(h):
        arrived(K_R, h)
        start(K_FWD, h)
        arrived(V_L, h)
        start(V_FWD, h)

    def forward_queries(h):
        arrived(Q_T, h)
        start(Q_FWD, h)
        arrived(G_T, h)
        start(G_FWD, h)

    prepare_keys(0)
    send_keys(0)
    prepare_queries(0)
    send_queries(0)
    for h in (1, 2):
        prepare_keys(h)
        prepare_queries(h)
    arrived(LEN_R, 0)
    start(LEN_FWD, 0)
    forward_keys(0)
    forward_queries(0)
    for h in (1, 2):
        send_values(h)
        send_keys(h)
        send_queries(h)
    arrived(LEN_L, 0)
    arrived(LEN_FWD, 0)

    def valid_row(slot):
        return (
            lax.broadcasted_iota(jnp.int32, (1, TOK), 1) < lens[slot][0:1, 0:1]
        ).astype(f32)

    def turn_keys(h, slot):
        valid = valid_row(slot)
        cols = rows(slot)
        ktbuf[:, cols] = (jnp.transpose(kbuf[h, cols, :].astype(f32)) * valid).astype(bf16)
        vtbuf[0:128, cols] = (jnp.transpose(vbuf[h, cols, :].astype(f32)) * valid).astype(bf16)
        vtbuf[128:144, cols] = jnp.broadcast_to(valid, (16, TOK)).astype(bf16)

    def forward_half(h, half):
        cols = pl.ds(half * HALF, HALF)
        query = qt[h, :, cols]
        top = None
        for slot in range(4):
            if half == 0:
                if slot == 1:
                    arrived(V_R, h)
                if slot == 2:
                    arrived(K_L, h)
                if slot == 3:
                    arrived(K_FWD, h)
            part = dot(kbuf[h, rows(slot), :], query, NN)
            score[rows(slot), :] = part
            part = jnp.max(part.reshape(TOK // 8, 8, HALF), axis=0)
            top = part if top is None else jnp.maximum(top, part)
        top = jnp.max(top, axis=0, keepdims=True) * SCALE_LOG2
        if half == 0:
            arrived(V_FWD, h)
            for slot in range(4):
                turn_keys(h, slot)
        for slot in range(4):
            prob[rows(slot), cols] = jnp.exp2(score[rows(slot), :] * SCALE_LOG2 - top).astype(bf16)
        out = dot(vtbuf[...], prob[:, cols], NN)
        oq_own[h, 0, :, cols] = out[0:128, :]
        inner = jnp.sum(out[0:128, :] * gt[h, :, cols].astype(f32), axis=0, keepdims=True)
        stat_out[h, 0:1, cols] = top
        stat_out[h, 1:2, cols] = out[128:129, :]
        stat_out[h, 2:3, cols] = inner

    def normalise(h):
        mine = stat_out[h]
        other = stat_in[h]
        other = jnp.concatenate(
            [other[:, TOK : 2 * TOK], other[:, 0:TOK], other[:, 3 * TOK :], other[:, 2 * TOK : 3 * TOK]],
            axis=1,
        )
        top = jnp.maximum(mine[0:1], other[0:1])
        grow_mine, grow_other = jnp.exp2(mine[0:1] - top), jnp.exp2(other[0:1] - top)
        inverse = 1.0 / (mine[1:2] * grow_mine + other[1:2] * grow_other)
        factor, factor_other = grow_mine * inverse, grow_other * inverse
        row_dot = (factor * mine[2:3] + factor_other * other[2:3]) * factor
        return factor, row_dot

    def share(h, which):
        oq_send[h, which, 0] = oq_own[h, which, :, TOK : 2 * TOK].astype(bf16)
        start((O_S1, DQ_S1)[which], h)
        oq_send[h, which, 1] = oq_own[h, which, :, 3 * TOK :].astype(bf16)
        start((O_S3, DQ_S3)[which], h)

    def pass_on(h, which):
        arrived((O_S3, DQ_S3)[which], h)
        both = oq_own[h, which, :, 2 * TOK : 3 * TOK] + oq_recv[h, which, 1].astype(f32)
        oq_send[h, which, 2] = both.astype(bf16)
        start((O_T, DQ_T)[which], h)

    def finish_queries(h, which):
        arrived((O_S1, DQ_S1)[which], h)
        arrived((O_T, DQ_T)[which], h)
        total = oq_own[h, which, :, 0:TOK] + oq_recv[h, which, 0].astype(f32)
        total = (total + oq_recv[h, which, 2].astype(f32)).astype(bf16).astype(f32)
        cols = slice(h * HEAD_DIM, (h + 1) * HEAD_DIM)
        if which == 0:
            o_out[0, :, cols] = jnp.transpose(jnp.where(present_cols, total, 0.0)).astype(bf16)
        else:
            dq_out[0, :, cols] = jnp.transpose(unrotate(total)).astype(bf16)

    def unrotate(total):
        cos, sin = tables[0:64, :], tables[64:128, :]
        d1, d2 = total[0:64, :], total[64:128, :]
        return jnp.concatenate([d1 * cos + d2 * sin, d2 * cos - d1 * sin], axis=0)

    def backward(h):
        factor, row_dot = normalise(h)
        gts[...] = (gt[h].astype(f32) * factor).astype(bf16)
        oq_own[h, 0] = oq_own[h, 0] * factor
        share(h, 0)
        for pair in (1, 0):
            keys = pl.ds(pair * HALF, HALF)
            value = vbuf[h, keys, :]
            for half in range(2):
                cols = pl.ds(half * HALF, HALF)
                grad = dot(value, gts[:, cols], NN)
                grad = prob[keys, cols].astype(f32) * (grad - row_dot[:, half * HALF : (half + 1) * HALF])
                dscore[keys, cols] = grad.astype(bf16)
            dv = dot(gts[...], prob[keys, :], NT)
            dk = dot(qt[h], dscore[keys, :], NT) * SCALE
            if pair == 1:
                kv_send[h, 0] = dk[:, TOK:].astype(bf16)
                start(DK3, h)
                kv_send[h, 1] = dv[:, TOK:].astype(bf16)
                start(DV3, h)
                kv_send[h, 2] = dv[:, 0:TOK].astype(bf16)
                start(DV2, h)
                kv_own[h, 2] = dk[:, 0:TOK]
            else:
                kv_send[h, 3] = dk[:, TOK:].astype(bf16)
                start(DK1, h)
                kv_own[h, 3] = dv[:, TOK:]
                kv_own[h, 0] = dk[:, 0:TOK]
                kv_own[h, 1] = dv[:, 0:TOK]
        oq_own[h, 1] = dot(ktbuf[...], dscore[...], NN) * SCALE
        share(h, 1)

    def reduce_keys(h):
        arrived(DK3, h)
        kv_send[h, 4] = (kv_own[h, 2] + kv_recv[h, 0].astype(f32)).astype(bf16)
        start(DK2, h)
        arrived(DV3, h)
        kv_send[h, 5] = (kv_own[h, 3] + kv_recv[h, 1].astype(f32)).astype(bf16)
        start(DV1, h)

    def finish_keys(h):
        cols = slice(h * HEAD_DIM, (h + 1) * HEAD_DIM)
        arrived(DK1, h)
        arrived(DK2, h)
        total = kv_own[h, 0] + kv_recv[h, 3].astype(f32) + kv_recv[h, 4].astype(f32)
        total = jnp.where(present_cols, total, 0.0).astype(bf16).astype(f32)
        dk_out[0, :, cols] = jnp.transpose(unrotate(total)).astype(bf16)
        arrived(DV2, h)
        arrived(DV1, h)
        total = kv_own[h, 1] + kv_recv[h, 2].astype(f32) + kv_recv[h, 5].astype(f32)
        dv_out[0, :, cols] = jnp.transpose(jnp.where(present_cols, total, 0.0)).astype(bf16)

    for h in range(HEADS_DEV):
        arrived(Q_S, h)
        arrived(G_S, h)
        forward_half(h, 0)
        if h > 0:
            pass_on(h - 1, 0)
            pass_on(h - 1, 1)
            reduce_keys(h - 1)
        if h + 1 < HEADS_DEV:
            forward_keys(h + 1)
            forward_queries(h + 1)
        arrived(Q_FWD, h)
        arrived(G_FWD, h)
        forward_half(h, 1)
        start(STATS, h)
        if h > 0:
            finish_queries(h - 1, 0)
            finish_queries(h - 1, 1)
            finish_keys(h - 1)
        arrived(STATS, h)
        backward(h)
    last = HEADS_DEV - 1
    pass_on(last, 0)
    reduce_keys(last)
    pass_on(last, 1)
    finish_queries(last, 0)
    finish_queries(last, 1)
    finish_keys(last)
    for h in range(HEADS_DEV):
        for kind in range(LEN_R):
            describe(kind, h).wait_send()
    for kind in (LEN_R, LEN_L, LEN_FWD):
        describe(kind, 0).wait_send()


def body(queries, key_input, values, cotangent, positions, lengths):
    rates = np.exp(-math.log(10000.0) * np.arange(64, dtype=np.float64) / 64).astype(np.float32)
    rates = jnp.asarray(np.broadcast_to(rates[:, None], (64, 128)))
    shape = jax.ShapeDtypeStruct(queries.shape, bf16)
    vmem = pl.BlockSpec(memory_space=pltpu.VMEM)
    block = (HEAD_DIM, TOK)
    n = HEADS_DEV
    return pl.pallas_call(
        kernel,
        out_shape=[shape] * 4,
        in_specs=[vmem] * 7,
        out_specs=[vmem] * 4,
        scratch_shapes=[
            pltpu.VMEM((n, ROWS, HEAD_DIM), bf16),
            pltpu.VMEM((n, ROWS, HEAD_DIM), bf16),
            pltpu.VMEM((HEAD_DIM, ROWS), bf16),
            pltpu.VMEM((HEAD_DIM + 16, ROWS), bf16),
            pltpu.VMEM((n, HEAD_DIM, ROWS), bf16),
            pltpu.VMEM((n, HEAD_DIM, ROWS), bf16),
            pltpu.VMEM((4, 8, 128), jnp.int32),
            pltpu.VMEM((ROWS, HALF), f32),
            pltpu.VMEM((ROWS, ROWS), bf16),
            pltpu.VMEM((ROWS, ROWS), bf16),
            pltpu.VMEM((HEAD_DIM, ROWS), bf16),
            pltpu.VMEM((n, 8, ROWS), f32),
            pltpu.VMEM((n, 8, ROWS), f32),
            pltpu.VMEM((n, 2, HEAD_DIM, ROWS), f32),
            pltpu.VMEM((n, 2, 3) + block, bf16),
            pltpu.VMEM((n, 2, 3) + block, bf16),
            pltpu.VMEM((n, 4) + block, f32),
            pltpu.VMEM((n, 6) + block, bf16),
            pltpu.VMEM((n, 6) + block, bf16),
            pltpu.VMEM(block, f32),
            pltpu.SemaphoreType.DMA((28, n)),
            pltpu.SemaphoreType.DMA((28, n)),
        ],
        compiler_params=pltpu.CompilerParams(
            collective_id=0, has_side_effects=True, vmem_limit_bytes=60 * 1024 * 1024
        ),
        cost_estimate=pl.CostEstimate(
            flops=12 * n * ROWS * ROWS * HEAD_DIM, bytes_accessed=16 << 20, transcendentals=n * ROWS * ROWS
        ),
        name="attention",
    )(queries, key_input, values, cotangent, positions, lengths, rates)


def solution(mesh):
    split = P("tower", "seq", "rep")
    return jax.shard_map(
        body,
        mesh=mesh,
        in_specs=(split, split, split, split, P("tower", "seq"), P("tower", "seq")),
        out_specs=(split, split, split, split),
        check_vma=False,
    )
```

```python
import math

import jax
import jax.numpy as jnp
from jax import lax
from jax.experimental import pallas as pl
from jax.experimental.pallas import tpu as pltpu
from jax.sharding import PartitionSpec as P

HEAD_DIM = 128
HEADS_DEV = 3
TOK = 384
ROWS = 4 * TOK
HALF = 2 * TOK
QCOLS = 12 * TOK
N_SEM = 80
SCALE = 1.0 / math.sqrt(HEAD_DIM)
SCALE_LOG2 = SCALE * math.log2(math.e)
MESH = pl.DeviceIdType.MESH
NN = (((1,), (0,)), ((), ()))
f32 = jnp.float32
bf16 = jnp.bfloat16


def dot(a, b):
    return lax.dot_general(a, b, NN, preferred_element_type=f32)


def rows(slot):
    return pl.ds(slot * TOK, TOK)


def kernel(
    q_hbm, k_hbm, v_hbm, g_hbm, pos_in, len_in,
    o_hbm, dq_hbm, dk_hbm, dv_hbm,
    ins, outs, in_sem, out_sem,
    khead, vhead, qhead, ghead,
    kbuf, vbuf, ktbuf, vtbuf, qt, gt, qr, gr, gts, lens,
    score, prob, dscore,
    stat_out, stat_in, oq_own, oq_send, oq_recv, oq_mate_send, oq_mate_recv,
    kv_own, kv_send, kv_recv, tables,
    send_sem, recv_sem,
):
    t, s, r = lax.axis_index("tower"), lax.axis_index("seq"), lax.axis_index("rep")
    x = s // 2
    odd = lax.rem(x, 2)
    mate = (t, s + 2 - 4 * odd, r)
    cross = (t, lax.rem(s + 6 + 4 * odd, 8), r)
    sibling = (t, s + 1 - 2 * lax.rem(s, 2), r)
    peer = (1 - t, s, r)
    mine = 2 * lax.rem((x + 1) // 2, 2)
    theirs = 2 - mine

    loads = {}
    for n, (name, src) in enumerate((("k", k_hbm), ("q", q_hbm), ("v", v_hbm), ("g", g_hbm))):
        loads[name] = pltpu.make_async_copy(src.at[0], ins.at[n], in_sem.at[n])
        loads[name].start()
    k_in, q_in, v_in, g_in = (ins.at[n] for n in range(4))
    stores = []

    def store(n, out, h, block):
        outs[n, :, head_cols(h)] = block
        copy = pltpu.make_async_copy(
            outs.at[n, :, head_cols(h)], out.at[0, :, head_cols(h)], out_sem.at[len(stores)]
        )
        copy.start()
        stores.append(copy)

    copies = {}

    def plan(name, src, dst, target):
        n = len(copies)
        copies[name] = pltpu.make_async_remote_copy(
            src_ref=src, dst_ref=dst, send_sem=send_sem.at[n], recv_sem=recv_sem.at[n],
            device_id=target, device_id_type=MESH,
        )

    def start(*names):
        for name in names:
            copies[name].start()

    def arrived(*names):
        for name in names:
            copies[name].wait_recv()

    plan("k_m", khead.at[theirs], kbuf.at[0, rows(1)], mate)
    plan("v_m", vhead.at[theirs], vbuf.at[0, rows(1)], mate)
    plan("q_m", qhead.at[theirs], qt.at[:, rows(4)], mate)
    plan("g_m", ghead.at[theirs], gt.at[:, rows(4)], mate)
    plan("k_c", khead.at[mine], kbuf.at[0, rows(2)], cross)
    plan("v_c", vhead.at[mine], vbuf.at[0, rows(2)], cross)
    plan("k_f", kbuf.at[0, rows(1)], kbuf.at[0, rows(3)], cross)
    plan("v_f", vbuf.at[0, rows(1)], vbuf.at[0, rows(3)], cross)
    plan("k1_m", khead.at[1], kbuf.at[1, rows(1)], mate)
    plan("v1_m", vhead.at[1], vbuf.at[1, rows(1)], mate)
    plan("k1_c", khead.at[1], kbuf.at[1, rows(2)], cross)
    plan("v1_c", vhead.at[1], vbuf.at[1, rows(2)], cross)
    plan("k1_f", kbuf.at[1, rows(1)], kbuf.at[1, rows(3)], cross)
    plan("v1_f", vbuf.at[1, rows(2)], vbuf.at[1, rows(3)], mate)
    plan("l_m", lens.at[0], lens.at[1], mate)
    plan("l_c", lens.at[0], lens.at[2], cross)
    plan("l_f", lens.at[1], lens.at[3], cross)
    for v in range(3):
        for name, buf in (("q", qt), ("g", gt)):
            plan((name + "_s", v), buf.at[:, rows(4 * v)], buf.at[:, rows(4 * v + 1)], sibling)
            plan((name + "_t", v), buf.at[:, rows(4 * v)], buf.at[:, rows(4 * v + 2)], peer)
            plan((name + "_f", v), buf.at[:, rows(4 * v + 2)], buf.at[:, rows(4 * v + 3)], sibling)
        for w in range(2):
            plan(("o_s1", v, w), oq_send.at[v, w, 0], oq_recv.at[v, w, 0], sibling)
            plan(("o_s3", v, w), oq_send.at[v, w, 1], oq_recv.at[v, w, 1], sibling)
            plan(("o_t", v, w), oq_send.at[v, w, 2], oq_recv.at[v, w, 2], peer)
    for half in range(6):
        plan(("st", half), stat_out.at[half], stat_in.at[half], sibling)
    for w in range(2):
        plan(("o_m", w), oq_mate_send.at[w], oq_mate_recv.at[w], mate)
        plan(("p2", w), kv_send.at[0, w, 0], kv_recv.at[0, w, 0], cross)
        plan(("p3", w), kv_send.at[0, w, 1], kv_recv.at[0, w, 1], cross)
        plan(("p1", w), kv_send.at[0, w, 2], kv_recv.at[0, w, 2], mate)
        plan(("s3", w), kv_send.at[1, w, 0], kv_recv.at[1, w, 0], (cross, mate)[w])
        plan(("s1", w), kv_send.at[1, w, 1], kv_recv.at[1, w, 1], mate)
        plan(("s2", w), kv_send.at[1, w, 2], kv_recv.at[1, w, 2], cross)

    barrier = pltpu.get_barrier_semaphore()
    for device in (mate, cross, sibling, peer):
        pl.semaphore_signal(barrier, inc=1, device_id=device, device_id_type=MESH)

    length = len_in[...]
    lens[0] = jnp.broadcast_to(length, (8, 128))
    exponent = lax.broadcasted_iota(jnp.int32, (64, TOK), 0).astype(f32)
    angles = jnp.exp(-math.log(10000.0) * exponent / 64) * pos_in[...].astype(f32)
    cos, sin = jnp.cos(angles), jnp.sin(angles)
    tables[0:64, :] = cos
    tables[64:128, :] = sin
    turned = jnp.transpose(tables[...])
    swapped = pltpu.roll(turned, 64, 1)
    low = lax.broadcasted_iota(jnp.int32, (TOK, HEAD_DIM), 1) < 64
    tables_rows = jnp.where(low, turned, swapped), jnp.where(low, -swapped, turned)
    present_rows = lax.broadcasted_iota(jnp.int32, (TOK, HEAD_DIM), 0) < length
    present_cols = lax.broadcasted_iota(jnp.int32, (1, TOK), 1) < length

    def prepare_keys(h):
        cos_rows, sin_rows = tables_rows
        key = k_in[:, h * HEAD_DIM : (h + 1) * HEAD_DIM].astype(f32)
        key = key * cos_rows + pltpu.roll(key, 64, 1) * sin_rows
        key = jnp.where(present_rows, key, key[0:1, :])
        khead[h] = key.astype(bf16)

    def prepare_queries(h):
        cols = slice(h * HEAD_DIM, (h + 1) * HEAD_DIM)
        query = jnp.transpose(q_in[:, cols].astype(f32))
        x1, x2 = query[0:64, :], query[64:128, :]
        qhead[h, 0:64, :] = (x1 * cos - x2 * sin).astype(bf16)
        qhead[h, 64:128, :] = (x2 * cos + x1 * sin).astype(bf16)
        grad = jnp.transpose(g_in[:, cols].astype(f32))
        ghead[h] = jnp.where(present_cols, grad, 0.0).astype(bf16)

    loads["k"].wait()
    prepare_keys(0)
    prepare_keys(2)
    pl.semaphore_wait(barrier, 4)
    start("k_m", "k_c", "l_m", "l_c")
    kbuf[0, 0:TOK, :] = khead[mine]
    loads["q"].wait()
    loads["g"].wait()
    prepare_queries(0)
    prepare_queries(2)
    start("q_m")
    qt[:, 0:TOK] = qhead[mine]
    start(("q_s", 0), ("q_t", 0))
    loads["v"].wait()
    for h in range(HEADS_DEV):
        vhead[h] = v_in[:, h * HEAD_DIM : (h + 1) * HEAD_DIM]
    start("v_m", "g_m")
    gt[:, 0:TOK] = ghead[mine]
    start(("g_s", 0), ("g_t", 0))
    vbuf[0, 0:TOK, :] = vhead[mine]
    arrived("l_m")
    start("l_f")

    def valid_row(slot):
        return (
            lax.broadcasted_iota(jnp.int32, (1, TOK), 1) < lens[slot][0:1, 0:1]
        ).astype(f32)

    def turn_keys(st, slot):
        valid = valid_row(slot)
        cols = rows(slot)
        ktbuf[st, :, cols] = (jnp.transpose(kbuf[st, cols, :].astype(f32)) * valid).astype(bf16)

    def turn_values(st, slot):
        valid = valid_row(slot)
        cols = rows(slot)
        vtbuf[st, 0:128, cols] = (jnp.transpose(vbuf[st, cols, :].astype(f32)) * valid).astype(bf16)
        vtbuf[st, 128:144, cols] = jnp.broadcast_to(valid, (16, TOK)).astype(bf16)

    def cols_of(half):
        return pl.ds(half * HALF, HALF)

    def prob_cols(half):
        return pl.ds((half % 4) * HALF, HALF)

    def scores(st, half, before=None):
        query = qt[:, cols_of(half)]
        top = None
        for slot in range(4):
            if before is not None:
                before(slot)
            part = dot(kbuf[st, rows(slot), :], query)
            score[half % 2, rows(slot), :] = part
            part = jnp.max(part.reshape(TOK // 8, 8, HALF), axis=0)
            top = part if top is None else jnp.maximum(top, part)
        top = jnp.max(top, axis=0, keepdims=True) * SCALE_LOG2
        stat_out[half, 0:1, :] = top
        for slot in range(4):
            prob[rows(slot), prob_cols(half)] = jnp.exp2(
                score[half % 2, rows(slot), :] * SCALE_LOG2 - top
            ).astype(bf16)

    def outputs(st, half):
        cols = cols_of(half)
        out = dot(vtbuf[st], prob[:, prob_cols(half)])
        oq_own[0, :, cols] = out[0:128, :]
        stat_out[half, 1:2, :] = out[128:129, :]
        stat_out[half, 2:3, :] = jnp.sum(
            out[0:128, :] * gt[:, cols].astype(f32), axis=0, keepdims=True
        )
        start(("st", half))

    def turn_queries(half):
        qr[cols_of(half), :] = jnp.transpose(qt[:, cols_of(half)].astype(f32)).astype(bf16)

    def normalise(half):
        arrived(("st", half))
        mine_, other = stat_out[half], stat_in[half]
        other = jnp.concatenate([other[:, TOK:], other[:, 0:TOK]], axis=1)
        top = jnp.maximum(mine_[0:1], other[0:1])
        grow, grow_other = jnp.exp2(mine_[0:1] - top), jnp.exp2(other[0:1] - top)
        inverse = 1.0 / (mine_[1:2] * grow + other[1:2] * grow_other)
        factor, factor_other = grow * inverse, grow_other * inverse
        row_dot = (factor * mine_[2:3] + factor_other * other[2:3]) * factor
        cols = cols_of(half)
        scaled = gt[:, cols].astype(f32) * factor
        gts[:, cols] = scaled.astype(bf16)
        gr[cols, :] = jnp.transpose(scaled).astype(bf16)
        oq_own[0, :, cols] = oq_own[0, :, cols] * factor
        return row_dot

    def share(v, w):
        oq_send[v, w, 0] = oq_own[w, :, rows(4 * v + 1)].astype(bf16)
        oq_send[v, w, 1] = oq_own[w, :, rows(4 * v + 3)].astype(bf16)
        start(("o_s3", v, w), ("o_s1", v, w))

    def pass_on(v, w):
        arrived(("o_s3", v, w))
        both = oq_own[w, :, rows(4 * v + 2)] + oq_recv[v, w, 1].astype(f32)
        oq_send[v, w, 2] = both.astype(bf16)
        start(("o_t", v, w))

    def total_queries(v, w):
        arrived(("o_s1", v, w), ("o_t", v, w))
        total = oq_own[w, :, rows(4 * v)] + oq_recv[v, w, 0].astype(f32)
        return (total + oq_recv[v, w, 2].astype(f32)).astype(bf16)

    def head_cols(h):
        if isinstance(h, int):
            return pl.ds(h * HEAD_DIM, HEAD_DIM)
        return pl.ds(pl.multiple_of(h * HEAD_DIM, HEAD_DIM), HEAD_DIM)

    def write_queries(h, w, total):
        total = total.astype(f32)
        if w == 0:
            total = jnp.where(present_cols, total, 0.0)
            store(0, o_hbm, h, jnp.transpose(total).astype(bf16))
        else:
            cos, sin = tables[0:64, :], tables[64:128, :]
            d1, d2 = total[0:64, :], total[64:128, :]
            total = jnp.concatenate([d1 * cos + d2 * sin, d2 * cos - d1 * sin], axis=0)
            store(1, dq_hbm, h, jnp.transpose(total).astype(bf16))

    def write_keys(h, w, total):
        total = jnp.where(present_rows, total.astype(f32), 0.0)
        if w == 0:
            cos_rows, sin_rows = tables_rows
            total = total.astype(bf16).astype(f32)
            total = total * cos_rows - pltpu.roll(total, 64, 1) * sin_rows
            store(2, dk_hbm, h, total.astype(bf16))
        else:
            store(3, dv_hbm, h, total.astype(bf16))

    def score_gradients(st, keys, half, row_dot):
        grad = dot(vbuf[st, keys, :], gts[:, cols_of(half)])
        grad = prob[keys, prob_cols(half)].astype(f32) * (grad - row_dot)
        dscore[keys, prob_cols(half)] = grad.astype(bf16)

    def key_gradients(st, keys, halves):
        width = pl.ds(0, len(halves) * HALF)
        queries = pl.ds(halves[0] * HALF, len(halves) * HALF)
        dk = dot(dscore[keys, width], qr[queries, :]) * SCALE
        dv = dot(prob[keys, width], gr[queries, :])
        return dk, dv

    def query_gradients(st, half):
        oq_own[1, :, cols_of(half)] = dot(ktbuf[st], dscore[:, prob_cols(half)]) * SCALE

    def relay(got, *onward):
        arrived(got)
        start(*onward)

    def before(slot):
        if slot == 1:
            relay("k_m", "k_f", "v_c")
        if slot == 2:
            relay(("q_t", 0), ("q_f", 0))
            arrived("k_c")
        if slot == 3:
            relay("q_m", ("q_s", 1), ("q_t", 1))
            arrived("k_f")

    arrived(("q_s", 0))
    scores(0, 0, before)
    relay("v_m", "v_f")
    prepare_keys(1)
    prepare_queries(1)
    kbuf[1, 0:TOK, :] = khead[1]
    vbuf[1, 0:TOK, :] = vhead[1]
    qt[:, 8 * TOK : 9 * TOK] = qhead[1]
    gt[:, 8 * TOK : 9 * TOK] = ghead[1]
    start("k1_m", "k1_c", "v1_m", "v1_c")
    relay(("g_t", 0), ("g_f", 0))
    arrived(("q_f", 0))
    scores(0, 1)
    arrived(("q_s", 1))
    scores(0, 2)
    relay("g_m", ("g_s", 1), ("g_t", 1))
    relay(("q_t", 1), ("q_f", 1))
    arrived("v_c", "l_c", "l_f", "v_f", ("g_s", 0), ("g_f", 0))
    for slot in range(4):
        turn_values(0, slot)
    outputs(0, 0)
    outputs(0, 1)
    start(("q_s", 2), ("q_t", 2), ("g_s", 2), ("g_t", 2))
    arrived(("q_f", 1))
    scores(0, 3)
    arrived(("g_s", 1))
    outputs(0, 2)
    relay(("g_t", 1), ("g_f", 1))
    for slot in range(4):
        turn_keys(0, slot)
    for half in range(4):
        turn_queries(half)
    arrived(("g_f", 1))
    outputs(0, 3)

    row_dots = [None] * 6
    for v in range(2):
        for half in (2 * v, 2 * v + 1):
            row_dots[half] = normalise(half)
        share(v, 0)
        for half in (2 * v, 2 * v + 1):
            score_gradients(0, pl.ds(HALF, HALF), half, row_dots[half])
    relay("k1_m", "k1_f")
    relay("v1_c", "v1_f")
    relay(("q_t", 2), ("q_f", 2))
    relay(("g_t", 2), ("g_f", 2))
    totals = key_gradients(0, pl.ds(HALF, HALF), (0, 1, 2, 3))
    for w in range(2):
        kv_send[0, w, 1] = totals[w][TOK:].astype(bf16)
        start(("p3", w))
    for w in range(2):
        kv_send[0, w, 0] = totals[w][0:TOK].astype(bf16)
        start(("p2", w))
    pass_on(0, 0)
    pass_on(1, 0)
    for half in range(4):
        score_gradients(0, pl.ds(0, HALF), half, row_dots[half])
    for half in (2, 3):
        query_gradients(0, half)
    share(1, 1)
    for half in (0, 1):
        query_gradients(0, half)
    share(0, 1)
    totals = key_gradients(0, pl.ds(0, HALF), (0, 1, 2, 3))
    pass_on(1, 1)
    pass_on(0, 1)
    for w, total in enumerate(totals):
        kv_own[0, w, 0] = total[0:TOK]
        kv_own[0, w, 1] = total[TOK:]

    arrived("k1_c", "k1_f", ("q_s", 2), ("q_f", 2))
    scores(1, 4)
    for w in range(2):
        arrived(("p3", w))
        kv_send[0, w, 2] = (kv_own[0, w, 1] + kv_recv[0, w, 1].astype(f32)).astype(bf16)
        start(("p1", w))
    scores(1, 5)
    oq_mate_send[0] = total_queries(1, 0)
    start(("o_m", 0))
    arrived("v1_m", "v1_f", ("g_s", 2), ("g_f", 2))
    for slot in range(4):
        turn_values(1, slot)
    outputs(1, 4)
    outputs(1, 5)
    for slot in range(4):
        turn_keys(1, slot)
    turn_queries(4)
    turn_queries(5)
    for w in range(2):
        arrived(("p2", w))
        write_keys(mine, w, (kv_own[0, w, 0] + kv_recv[0, w, 0].astype(f32)).astype(bf16))
    write_queries(mine, 0, total_queries(0, 0))

    for half in (4, 5):
        row_dots[half] = normalise(half)
    share(2, 0)

    def gradients(slot):
        for half in (4, 5):
            score_gradients(1, rows(slot), half, row_dots[half])

    def gather_gradients(slot):
        return key_gradients(1, rows(slot), (4, 5))

    gradients(3)
    dk, dv = gather_gradients(3)
    kv_send[1, 0, 0] = dk.astype(bf16)
    start(("s3", 0))
    kv_send[1, 1, 0] = dv.astype(bf16)
    start(("s3", 1))
    gradients(2)
    dk, dv = gather_gradients(2)
    kv_send[1, 0, 2] = dk.astype(bf16)
    start(("s2", 0))
    kv_own[1, 1, 1] = dv
    pass_on(2, 0)
    oq_mate_send[1] = total_queries(1, 1)
    start(("o_m", 1))
    gradients(1)
    gradients(0)
    for half in (4, 5):
        query_gradients(1, half)
    share(2, 1)
    dk, dv = gather_gradients(1)
    kv_send[1, 1, 1] = dv.astype(bf16)
    start(("s1", 1))
    arrived(("s3", 0))
    kv_send[1, 0, 1] = (dk + kv_recv[1, 0, 0].astype(f32)).astype(bf16)
    start(("s1", 0))
    arrived(("s3", 1))
    kv_send[1, 1, 2] = (kv_own[1, 1, 1] + kv_recv[1, 1, 0].astype(f32)).astype(bf16)
    start(("s2", 1))
    dk, dv = gather_gradients(0)
    pass_on(2, 1)
    kv_own[1, 0, 0] = dk
    kv_own[1, 1, 0] = dv

    write_queries(mine, 1, total_queries(0, 1))
    for w in range(2):
        arrived(("p1", w))
        write_keys(theirs, w, kv_recv[0, w, 2])
    for w in range(2):
        arrived(("o_m", w))
        write_queries(theirs, w, oq_mate_recv[w])
    write_queries(1, 0, total_queries(2, 0))
    for w in (1, 0):
        arrived(("s1", w), ("s2", w))
        total = kv_own[1, w, 0] + kv_recv[1, w, 1].astype(f32) + kv_recv[1, w, 2].astype(f32)
        write_keys(1, w, total.astype(bf16))
    write_queries(1, 1, total_queries(2, 1))
    for copy in stores:
        copy.wait()
    for copy in copies.values():
        copy.wait_send()


def hand_over(*refs):
    sources, results, (held, load_sem, store_sem) = refs[:4], refs[4:8], refs[8:]
    loads = [pltpu.make_async_copy(sources[n], held.at[n], load_sem.at[n]) for n in range(4)]
    stores = [pltpu.make_async_copy(held.at[n], results[n], store_sem.at[n]) for n in range(4)]
    for copy in loads:
        copy.start()
    for load, copy in zip(loads, stores):
        load.wait()
        copy.start()
    for copy in stores:
        copy.wait()


def body(queries, key_input, values, cotangent, positions, lengths):
    shape = jax.ShapeDtypeStruct(queries.shape, bf16)
    vmem = pl.BlockSpec(memory_space=pltpu.VMEM)
    hbm = pl.BlockSpec(memory_space=pl.ANY)
    tokens, turned = (TOK, HEAD_DIM), (HEAD_DIM, TOK)
    n = HEADS_DEV
    results = pl.pallas_call(
        kernel,
        out_shape=[shape] * 4,
        in_specs=[hbm] * 4 + [vmem] * 2,
        out_specs=[hbm] * 4,
        scratch_shapes=[
            pltpu.VMEM((4, TOK, HEADS_DEV * HEAD_DIM), bf16),
            pltpu.VMEM((4, TOK, HEADS_DEV * HEAD_DIM), bf16),
            pltpu.SemaphoreType.DMA((4,)),
            pltpu.SemaphoreType.DMA((12,)),
            pltpu.VMEM((n,) + tokens, bf16),
            pltpu.VMEM((n,) + tokens, bf16),
            pltpu.VMEM((n,) + turned, bf16),
            pltpu.VMEM((n,) + turned, bf16),
            pltpu.VMEM((2, ROWS, HEAD_DIM), bf16),
            pltpu.VMEM((2, ROWS, HEAD_DIM), bf16),
            pltpu.VMEM((2, HEAD_DIM, ROWS), bf16),
            pltpu.VMEM((2, HEAD_DIM + 16, ROWS), bf16),
            pltpu.VMEM((HEAD_DIM, QCOLS), bf16),
            pltpu.VMEM((HEAD_DIM, QCOLS), bf16),
            pltpu.VMEM((QCOLS, HEAD_DIM), bf16),
            pltpu.VMEM((QCOLS, HEAD_DIM), bf16),
            pltpu.VMEM((HEAD_DIM, QCOLS), bf16),
            pltpu.VMEM((4, 8, 128), jnp.int32),
            pltpu.VMEM((2, ROWS, HALF), f32),
            pltpu.VMEM((ROWS, 4 * HALF), bf16),
            pltpu.VMEM((ROWS, 4 * HALF), bf16),
            pltpu.VMEM((6, 8, HALF), f32),
            pltpu.VMEM((6, 8, HALF), f32),
            pltpu.VMEM((2, HEAD_DIM, QCOLS), f32),
            pltpu.VMEM((n, 2, 3) + turned, bf16),
            pltpu.VMEM((n, 2, 3) + turned, bf16),
            pltpu.VMEM((2,) + turned, bf16),
            pltpu.VMEM((2,) + turned, bf16),
            pltpu.VMEM((2, 2, 2) + tokens, f32),
            pltpu.VMEM((2, 2, 3) + tokens, bf16),
            pltpu.VMEM((2, 2, 3) + tokens, bf16),
            pltpu.VMEM(turned, f32),
            pltpu.SemaphoreType.DMA((N_SEM,)),
            pltpu.SemaphoreType.DMA((N_SEM,)),
        ],
        compiler_params=pltpu.CompilerParams(
            collective_id=0, has_side_effects=True, vmem_limit_bytes=60 * 1024 * 1024
        ),
        cost_estimate=pl.CostEstimate(
            flops=12 * n * ROWS * ROWS * HEAD_DIM, bytes_accessed=16 << 20, transcendentals=n * ROWS * ROWS
        ),
        name="attention",
    )(queries, key_input, values, cotangent, positions, lengths)
    return pl.pallas_call(
        hand_over,
        out_shape=[shape] * 4,
        in_specs=[hbm] * 4,
        out_specs=[hbm] * 4,
        scratch_shapes=[
            pltpu.VMEM((4, 1, TOK, HEADS_DEV * HEAD_DIM), bf16),
            pltpu.SemaphoreType.DMA((4,)),
            pltpu.SemaphoreType.DMA((4,)),
        ],
        name="hand_over",
    )(*results)


def solution(mesh):
    split = P("tower", "seq", "rep")
    return jax.shard_map(
        body,
        mesh=mesh,
        in_specs=(split, split, split, split, P("tower", "seq"), P("tower", "seq")),
        out_specs=(split, split, split, split),
        check_vma=False,
    )
```

```python
import math

import jax
import jax.numpy as jnp
from jax import lax
from jax.experimental import pallas as pl
from jax.experimental.pallas import tpu as pltpu
from jax.sharding import PartitionSpec as P

HEAD_DIM = 128
HEADS_DEV = 3
TOK = 384
ROWS = 4 * TOK
HALF = 2 * TOK
QCOLS = 12 * TOK
N_SEM = 80
SCALE = 1.0 / math.sqrt(HEAD_DIM)
SCALE_LOG2 = SCALE * math.log2(math.e)
MESH = pl.DeviceIdType.MESH
NN = (((1,), (0,)), ((), ()))
f32 = jnp.float32
bf16 = jnp.bfloat16


def dot(a, b):
    return lax.dot_general(a, b, NN, preferred_element_type=f32)


def rows(slot):
    return pl.ds(slot * TOK, TOK)


def kernel(
    q_hbm, k_hbm, v_hbm, g_hbm, pos_in, len_in,
    o_hbm, dq_hbm, dk_hbm, dv_hbm,
    ins, outs, in_sem, out_sem,
    khead, vhead, qhead, ghead,
    kbuf, vbuf, ktbuf, vtbuf, qt, gt, qr, gr, gts, lens,
    score, prob, dscore,
    stat_out, stat_in, oq_own, oq_send, oq_recv, oq_mate_send, oq_mate_recv,
    kv_own, kv_send, kv_recv, tables,
    send_sem, recv_sem,
):
    t, s, r = lax.axis_index("tower"), lax.axis_index("seq"), lax.axis_index("rep")
    x = s // 2
    odd = lax.rem(x, 2)
    mate = (t, s + 2 - 4 * odd, r)
    cross = (t, lax.rem(s + 6 + 4 * odd, 8), r)
    sibling = (t, s + 1 - 2 * lax.rem(s, 2), r)
    peer = (1 - t, s, r)
    mine = 2 * lax.rem((x + 1) // 2, 2)
    theirs = 2 - mine

    loads = {}
    for n, (name, src) in enumerate((("k", k_hbm), ("q", q_hbm), ("v", v_hbm), ("g", g_hbm))):
        loads[name] = pltpu.make_async_copy(src.at[0], ins.at[n], in_sem.at[n])
        loads[name].start()
    k_in, q_in, v_in, g_in = (ins.at[n] for n in range(4))
    stores = []

    def store(n, out, h, block):
        outs[n, :, head_cols(h)] = block
        copy = pltpu.make_async_copy(
            outs.at[n, :, head_cols(h)], out.at[0, :, head_cols(h)], out_sem.at[len(stores)]
        )
        copy.start()
        stores.append(copy)

    copies = {}

    def plan(name, src, dst, target):
        n = len(copies)
        copies[name] = pltpu.make_async_remote_copy(
            src_ref=src, dst_ref=dst, send_sem=send_sem.at[n], recv_sem=recv_sem.at[n],
            device_id=target, device_id_type=MESH,
        )

    def start(*names):
        for name in names:
            copies[name].start()

    def arrived(*names):
        for name in names:
            copies[name].wait_recv()

    for n in range(2):
        part = pl.ds(n * TOK // 2, TOK // 2)
        first, third = pl.ds(TOK + n * TOK // 2, TOK // 2), pl.ds(3 * TOK + n * TOK // 2, TOK // 2)
        for name, head, buf in (("k", khead, kbuf), ("v", vhead, vbuf)):
            plan((name + "_m", n), head.at[theirs, part], buf.at[0, first], mate)
            plan((name + "_f", n), buf.at[0, first], buf.at[0, third], cross)
    plan("q_m", qhead.at[theirs], qt.at[:, rows(4)], mate)
    plan("g_m", ghead.at[theirs], gt.at[:, rows(4)], mate)
    plan("k_c", khead.at[mine], kbuf.at[0, rows(2)], cross)
    plan("v_c", vhead.at[mine], vbuf.at[0, rows(2)], cross)
    plan("k1_m", khead.at[1], kbuf.at[1, rows(1)], mate)
    plan("v1_m", vhead.at[1], vbuf.at[1, rows(1)], mate)
    plan("k1_c", khead.at[1], kbuf.at[1, rows(2)], cross)
    plan("v1_c", vhead.at[1], vbuf.at[1, rows(2)], cross)
    plan("k1_f", kbuf.at[1, rows(1)], kbuf.at[1, rows(3)], cross)
    plan("v1_f", vbuf.at[1, rows(2)], vbuf.at[1, rows(3)], mate)
    plan("l_m", lens.at[0], lens.at[1], mate)
    plan("l_c", lens.at[0], lens.at[2], cross)
    plan("l_f", lens.at[1], lens.at[3], cross)
    for v in range(3):
        for name, buf in (("q", qt), ("g", gt)):
            plan((name + "_s", v), buf.at[:, rows(4 * v)], buf.at[:, rows(4 * v + 1)], sibling)
            plan((name + "_t", v), buf.at[:, rows(4 * v)], buf.at[:, rows(4 * v + 2)], peer)
            plan((name + "_f", v), buf.at[:, rows(4 * v + 2)], buf.at[:, rows(4 * v + 3)], sibling)
        for w in range(2):
            plan(("o_s1", v, w), oq_send.at[v, w, 0], oq_recv.at[v, w, 0], sibling)
            plan(("o_s3", v, w), oq_send.at[v, w, 1], oq_recv.at[v, w, 1], sibling)
            plan(("o_t", v, w), oq_send.at[v, w, 2], oq_recv.at[v, w, 2], peer)
    for half in range(6):
        plan(("st", half), stat_out.at[half], stat_in.at[half], sibling)
    for w in range(2):
        plan(("o_m", w), oq_mate_send.at[w], oq_mate_recv.at[w], mate)
        plan(("p2", w), kv_send.at[0, w, 0], kv_recv.at[0, w, 0], cross)
        plan(("p3", w), kv_send.at[0, w, 1], kv_recv.at[0, w, 1], cross)
        plan(("p1", w), kv_send.at[0, w, 2], kv_recv.at[0, w, 2], mate)
        plan(("s3", w), kv_send.at[1, w, 0], kv_recv.at[1, w, 0], (cross, mate)[w])
        plan(("s1", w), kv_send.at[1, w, 1], kv_recv.at[1, w, 1], mate)
        plan(("s2", w), kv_send.at[1, w, 2], kv_recv.at[1, w, 2], cross)

    barrier = pltpu.get_barrier_semaphore()
    for device in (mate, cross, sibling, peer):
        pl.semaphore_signal(barrier, inc=1, device_id=device, device_id_type=MESH)

    length = len_in[...]
    lens[0] = jnp.broadcast_to(length, (8, 128))
    exponent = lax.broadcasted_iota(jnp.int32, (64, TOK), 0).astype(f32)
    angles = jnp.exp(-math.log(10000.0) * exponent / 64) * pos_in[...].astype(f32)
    cos, sin = jnp.cos(angles), jnp.sin(angles)
    tables[0:64, :] = cos
    tables[64:128, :] = sin
    turned = jnp.transpose(tables[...])
    swapped = pltpu.roll(turned, 64, 1)
    low = lax.broadcasted_iota(jnp.int32, (TOK, HEAD_DIM), 1) < 64
    tables_rows = jnp.where(low, turned, swapped), jnp.where(low, -swapped, turned)
    present_rows = lax.broadcasted_iota(jnp.int32, (TOK, HEAD_DIM), 0) < length
    present_cols = lax.broadcasted_iota(jnp.int32, (1, TOK), 1) < length

    def prepare_keys(h):
        cos_rows, sin_rows = tables_rows
        key = k_in[:, h * HEAD_DIM : (h + 1) * HEAD_DIM].astype(f32)
        key = key * cos_rows + pltpu.roll(key, 64, 1) * sin_rows
        key = jnp.where(present_rows, key, key[0:1, :])
        khead[h] = key.astype(bf16)

    def prepare_queries(h):
        cols = slice(h * HEAD_DIM, (h + 1) * HEAD_DIM)
        query = jnp.transpose(q_in[:, cols].astype(f32))
        x1, x2 = query[0:64, :], query[64:128, :]
        qhead[h, 0:64, :] = (x1 * cos - x2 * sin).astype(bf16)
        qhead[h, 64:128, :] = (x2 * cos + x1 * sin).astype(bf16)
        grad = jnp.transpose(g_in[:, cols].astype(f32))
        ghead[h] = jnp.where(present_cols, grad, 0.0).astype(bf16)

    loads["k"].wait()
    prepare_keys(0)
    prepare_keys(2)
    pl.semaphore_wait(barrier, 4)
    start(("k_m", 0), ("k_m", 1), "k_c", "l_m", "l_c")
    kbuf[0, 0:TOK, :] = khead[mine]
    loads["q"].wait()
    loads["g"].wait()
    prepare_queries(0)
    prepare_queries(2)
    start("q_m")
    qt[:, 0:TOK] = qhead[mine]
    start(("q_s", 0), ("q_t", 0))
    loads["v"].wait()
    for h in range(HEADS_DEV):
        vhead[h] = v_in[:, h * HEAD_DIM : (h + 1) * HEAD_DIM]
    start(("v_m", 0), ("v_m", 1), "g_m")
    gt[:, 0:TOK] = ghead[mine]
    start(("g_s", 0), ("g_t", 0))
    vbuf[0, 0:TOK, :] = vhead[mine]

    def valid_row(slot):
        return (
            lax.broadcasted_iota(jnp.int32, (1, TOK), 1) < lens[slot][0:1, 0:1]
        ).astype(f32)

    def turn_keys(st, slot):
        valid = valid_row(slot)
        cols = rows(slot)
        ktbuf[st, :, cols] = (jnp.transpose(kbuf[st, cols, :].astype(f32)) * valid).astype(bf16)

    def turn_values(st, slot):
        valid = valid_row(slot)
        cols = rows(slot)
        vtbuf[st, 0:128, cols] = (jnp.transpose(vbuf[st, cols, :].astype(f32)) * valid).astype(bf16)
        vtbuf[st, 128:144, cols] = jnp.broadcast_to(valid, (16, TOK)).astype(bf16)

    def cols_of(half):
        return pl.ds(half * HALF, HALF)

    def prob_cols(half):
        return pl.ds((half % 4) * HALF, HALF)

    def scores(st, half, before=None):
        query = qt[:, cols_of(half)]
        top = None
        for slot in range(4):
            if before is not None:
                before(slot)
            part = dot(kbuf[st, rows(slot), :], query)
            score[half % 2, rows(slot), :] = part
            part = jnp.max(part.reshape(TOK // 8, 8, HALF), axis=0)
            top = part if top is None else jnp.maximum(top, part)
        top = jnp.max(top, axis=0, keepdims=True) * SCALE_LOG2
        stat_out[half, 0:1, :] = top
        for slot in range(4):
            prob[rows(slot), prob_cols(half)] = jnp.exp2(
                score[half % 2, rows(slot), :] * SCALE_LOG2 - top
            ).astype(bf16)

    def outputs(st, half):
        cols = cols_of(half)
        out = dot(vtbuf[st], prob[:, prob_cols(half)])
        oq_own[0, :, cols] = out[0:128, :]
        stat_out[half, 1:2, :] = out[128:129, :]

    def send_stats(half):
        cols = cols_of(half)
        stat_out[half, 2:3, :] = jnp.sum(
            oq_own[0, :, cols] * gt[:, cols].astype(f32), axis=0, keepdims=True
        )
        start(("st", half))

    def turn_queries(half):
        qr[cols_of(half), :] = jnp.transpose(qt[:, cols_of(half)].astype(f32)).astype(bf16)

    def normalise(half):
        arrived(("st", half))
        mine_, other = stat_out[half], stat_in[half]
        other = jnp.concatenate([other[:, TOK:], other[:, 0:TOK]], axis=1)
        top = jnp.maximum(mine_[0:1], other[0:1])
        grow, grow_other = jnp.exp2(mine_[0:1] - top), jnp.exp2(other[0:1] - top)
        inverse = 1.0 / (mine_[1:2] * grow + other[1:2] * grow_other)
        factor, factor_other = grow * inverse, grow_other * inverse
        row_dot = (factor * mine_[2:3] + factor_other * other[2:3]) * factor
        cols = cols_of(half)
        scaled = gt[:, cols].astype(f32) * factor
        gts[:, cols] = scaled.astype(bf16)
        gr[cols, :] = jnp.transpose(scaled).astype(bf16)
        oq_own[0, :, cols] = oq_own[0, :, cols] * factor
        return row_dot

    def share(v, w):
        oq_send[v, w, 0] = oq_own[w, :, rows(4 * v + 1)].astype(bf16)
        oq_send[v, w, 1] = oq_own[w, :, rows(4 * v + 3)].astype(bf16)
        start(("o_s3", v, w), ("o_s1", v, w))

    def pass_on(v, w):
        arrived(("o_s3", v, w))
        both = oq_own[w, :, rows(4 * v + 2)] + oq_recv[v, w, 1].astype(f32)
        oq_send[v, w, 2] = both.astype(bf16)
        start(("o_t", v, w))

    def total_queries(v, w):
        arrived(("o_s1", v, w), ("o_t", v, w))
        total = oq_own[w, :, rows(4 * v)] + oq_recv[v, w, 0].astype(f32)
        return (total + oq_recv[v, w, 2].astype(f32)).astype(bf16)

    def head_cols(h):
        if isinstance(h, int):
            return pl.ds(h * HEAD_DIM, HEAD_DIM)
        return pl.ds(pl.multiple_of(h * HEAD_DIM, HEAD_DIM), HEAD_DIM)

    def write_queries(h, w, total):
        total = total.astype(f32)
        if w == 0:
            total = jnp.where(present_cols, total, 0.0)
            store(0, o_hbm, h, jnp.transpose(total).astype(bf16))
        else:
            cos, sin = tables[0:64, :], tables[64:128, :]
            d1, d2 = total[0:64, :], total[64:128, :]
            total = jnp.concatenate([d1 * cos + d2 * sin, d2 * cos - d1 * sin], axis=0)
            store(1, dq_hbm, h, jnp.transpose(total).astype(bf16))

    def write_keys(h, w, total):
        total = jnp.where(present_rows, total.astype(f32), 0.0)
        if w == 0:
            cos_rows, sin_rows = tables_rows
            total = total.astype(bf16).astype(f32)
            total = total * cos_rows - pltpu.roll(total, 64, 1) * sin_rows
            store(2, dk_hbm, h, total.astype(bf16))
        else:
            store(3, dv_hbm, h, total.astype(bf16))

    def score_gradients(st, keys, half, row_dot):
        grad = dot(vbuf[st, keys, :], gts[:, cols_of(half)])
        grad = prob[keys, prob_cols(half)].astype(f32) * (grad - row_dot)
        dscore[keys, prob_cols(half)] = grad.astype(bf16)

    def key_gradients(st, keys, halves):
        width = pl.ds(0, len(halves) * HALF)
        queries = pl.ds(halves[0] * HALF, len(halves) * HALF)
        dk = dot(dscore[keys, width], qr[queries, :]) * SCALE
        dv = dot(prob[keys, width], gr[queries, :])
        return dk, dv

    def query_gradients(st, half):
        oq_own[1, :, cols_of(half)] = dot(ktbuf[st], dscore[:, prob_cols(half)]) * SCALE

    def relay(got, *onward):
        arrived(got)
        start(*onward)

    def before(slot):
        if slot == 2:
            relay(("q_t", 0), ("q_f", 0))
            arrived("k_c")
        if slot == 3:
            relay("q_m", ("q_s", 1), ("q_t", 1))
            arrived(("k_f", 0), ("k_f", 1))

    relay(("k_m", 0), ("k_f", 0))
    relay(("k_m", 1), ("k_f", 1), "v_c")
    relay("l_m", "l_f")
    arrived(("q_s", 0))
    scores(0, 0, before)
    relay(("v_m", 0), ("v_f", 0))
    relay(("v_m", 1), ("v_f", 1))
    prepare_keys(1)
    kbuf[1, 0:TOK, :] = khead[1]
    vbuf[1, 0:TOK, :] = vhead[1]
    start("k1_m", "k1_c", "v1_m", "v1_c")
    arrived(("q_f", 0))
    scores(0, 1)
    relay(("g_t", 0), ("g_f", 0))
    arrived(("q_s", 1))
    scores(0, 2)
    relay(("q_t", 1), ("q_f", 1))
    relay("g_m", ("g_s", 1), ("g_t", 1))
    prepare_queries(1)
    qt[:, 8 * TOK : 9 * TOK] = qhead[1]
    gt[:, 8 * TOK : 9 * TOK] = ghead[1]
    start(("q_s", 2), ("q_t", 2), ("g_s", 2), ("g_t", 2))
    arrived("v_c", "l_c", "l_f", ("v_f", 0), ("v_f", 1))
    for slot in range(4):
        turn_values(0, slot)
    outputs(0, 0)
    outputs(0, 1)
    arrived(("g_s", 0), ("g_f", 0))
    send_stats(0)
    send_stats(1)
    arrived(("q_f", 1))
    scores(0, 3)
    for slot in range(4):
        turn_keys(0, slot)
    for half in range(4):
        turn_queries(half)
    outputs(0, 2)
    outputs(0, 3)

    near, far = pl.ds(0, HALF), pl.ds(HALF, HALF)
    row_dots = [None] * 6
    for half in (0, 1):
        row_dots[half] = normalise(half)
    share(0, 0)
    for half in (0, 1):
        score_gradients(0, far, half, row_dots[half])
    relay(("g_t", 1), ("g_f", 1))
    arrived(("g_s", 1))
    send_stats(2)
    for half in (0, 1):
        score_gradients(0, near, half, row_dots[half])
    arrived(("g_f", 1))
    send_stats(3)
    pass_on(0, 0)
    for half in (0, 1):
        query_gradients(0, half)
    share(0, 1)
    relay("k1_m", "k1_f")
    relay("v1_c", "v1_f")
    for half in (2, 3):
        row_dots[half] = normalise(half)
    share(1, 0)
    for half in (2, 3):
        score_gradients(0, far, half, row_dots[half])
    totals = key_gradients(0, far, (0, 1, 2, 3))
    for w in range(2):
        kv_send[0, w, 1] = totals[w][TOK:].astype(bf16)
        start(("p3", w))
    for w in range(2):
        kv_send[0, w, 0] = totals[w][0:TOK].astype(bf16)
        start(("p2", w))
    pass_on(1, 0)
    relay(("q_t", 2), ("q_f", 2))
    relay(("g_t", 2), ("g_f", 2))
    for half in (2, 3):
        score_gradients(0, near, half, row_dots[half])
    for half in (2, 3):
        query_gradients(0, half)
    share(1, 1)
    pass_on(0, 1)
    totals = key_gradients(0, near, (0, 1, 2, 3))
    pass_on(1, 1)
    for w, total in enumerate(totals):
        kv_own[0, w, 0] = total[0:TOK]
        kv_own[0, w, 1] = total[TOK:]

    arrived("k1_c", "k1_f", ("q_s", 2), ("q_f", 2))
    scores(1, 4)
    for w in range(2):
        arrived(("p3", w))
        kv_send[0, w, 2] = (kv_own[0, w, 1] + kv_recv[0, w, 1].astype(f32)).astype(bf16)
        start(("p1", w))
    scores(1, 5)
    oq_mate_send[0] = total_queries(1, 0)
    start(("o_m", 0))
    arrived("v1_m", "v1_f", ("g_s", 2), ("g_f", 2))
    for slot in range(4):
        turn_values(1, slot)
    outputs(1, 4)
    send_stats(4)
    outputs(1, 5)
    send_stats(5)
    for slot in range(4):
        turn_keys(1, slot)
    turn_queries(4)
    turn_queries(5)
    for w in range(2):
        arrived(("p2", w))
        write_keys(mine, w, (kv_own[0, w, 0] + kv_recv[0, w, 0].astype(f32)).astype(bf16))
    write_queries(mine, 0, total_queries(0, 0))

    for half in (4, 5):
        row_dots[half] = normalise(half)
    share(2, 0)

    def gradients(slot):
        for half in (4, 5):
            score_gradients(1, rows(slot), half, row_dots[half])

    def gather_gradients(slot):
        return key_gradients(1, rows(slot), (4, 5))

    gradients(3)
    dk, dv = gather_gradients(3)
    kv_send[1, 0, 0] = dk.astype(bf16)
    start(("s3", 0))
    kv_send[1, 1, 0] = dv.astype(bf16)
    start(("s3", 1))
    gradients(2)
    dk, dv = gather_gradients(2)
    kv_send[1, 0, 2] = dk.astype(bf16)
    start(("s2", 0))
    kv_own[1, 1, 1] = dv
    pass_on(2, 0)
    oq_mate_send[1] = total_queries(1, 1)
    start(("o_m", 1))
    gradients(1)
    gradients(0)
    for half in (4, 5):
        query_gradients(1, half)
    share(2, 1)
    dk, dv = gather_gradients(1)
    kv_send[1, 1, 1] = dv.astype(bf16)
    start(("s1", 1))
    arrived(("s3", 0))
    kv_send[1, 0, 1] = (dk + kv_recv[1, 0, 0].astype(f32)).astype(bf16)
    start(("s1", 0))
    arrived(("s3", 1))
    kv_send[1, 1, 2] = (kv_own[1, 1, 1] + kv_recv[1, 1, 0].astype(f32)).astype(bf16)
    start(("s2", 1))
    dk, dv = gather_gradients(0)
    pass_on(2, 1)
    kv_own[1, 0, 0] = dk
    kv_own[1, 1, 0] = dv

    write_queries(mine, 1, total_queries(0, 1))
    for w in range(2):
        arrived(("p1", w))
        write_keys(theirs, w, kv_recv[0, w, 2])
    for w in range(2):
        arrived(("o_m", w))
        write_queries(theirs, w, oq_mate_recv[w])
    write_queries(1, 0, total_queries(2, 0))
    for w in (1, 0):
        arrived(("s1", w), ("s2", w))
        total = kv_own[1, w, 0] + kv_recv[1, w, 1].astype(f32) + kv_recv[1, w, 2].astype(f32)
        write_keys(1, w, total.astype(bf16))
    write_queries(1, 1, total_queries(2, 1))
    for copy in stores:
        copy.wait()
    for copy in copies.values():
        copy.wait_send()


def hand_over(*refs):
    sources, results, (held, load_sem, store_sem) = refs[:4], refs[4:8], refs[8:]
    loads = [pltpu.make_async_copy(sources[n], held.at[n], load_sem.at[n]) for n in range(4)]
    stores = [pltpu.make_async_copy(held.at[n], results[n], store_sem.at[n]) for n in range(4)]
    for copy in loads:
        copy.start()
    for load, copy in zip(loads, stores):
        load.wait()
        copy.start()
    for copy in stores:
        copy.wait()


def body(queries, key_input, values, cotangent, positions, lengths):
    shape = jax.ShapeDtypeStruct(queries.shape, bf16)
    vmem = pl.BlockSpec(memory_space=pltpu.VMEM)
    hbm = pl.BlockSpec(memory_space=pl.ANY)
    tokens, turned = (TOK, HEAD_DIM), (HEAD_DIM, TOK)
    n = HEADS_DEV
    results = pl.pallas_call(
        kernel,
        out_shape=[shape] * 4,
        in_specs=[hbm] * 4 + [vmem] * 2,
        out_specs=[hbm] * 4,
        scratch_shapes=[
            pltpu.VMEM((4, TOK, HEADS_DEV * HEAD_DIM), bf16),
            pltpu.VMEM((4, TOK, HEADS_DEV * HEAD_DIM), bf16),
            pltpu.SemaphoreType.DMA((4,)),
            pltpu.SemaphoreType.DMA((12,)),
            pltpu.VMEM((n,) + tokens, bf16),
            pltpu.VMEM((n,) + tokens, bf16),
            pltpu.VMEM((n,) + turned, bf16),
            pltpu.VMEM((n,) + turned, bf16),
            pltpu.VMEM((2, ROWS, HEAD_DIM), bf16),
            pltpu.VMEM((2, ROWS, HEAD_DIM), bf16),
            pltpu.VMEM((2, HEAD_DIM, ROWS), bf16),
            pltpu.VMEM((2, HEAD_DIM + 16, ROWS), bf16),
            pltpu.VMEM((HEAD_DIM, QCOLS), bf16),
            pltpu.VMEM((HEAD_DIM, QCOLS), bf16),
            pltpu.VMEM((QCOLS, HEAD_DIM), bf16),
            pltpu.VMEM((QCOLS, HEAD_DIM), bf16),
            pltpu.VMEM((HEAD_DIM, QCOLS), bf16),
            pltpu.VMEM((4, 8, 128), jnp.int32),
            pltpu.VMEM((2, ROWS, HALF), f32),
            pltpu.VMEM((ROWS, 4 * HALF), bf16),
            pltpu.VMEM((ROWS, 4 * HALF), bf16),
            pltpu.VMEM((6, 8, HALF), f32),
            pltpu.VMEM((6, 8, HALF), f32),
            pltpu.VMEM((2, HEAD_DIM, QCOLS), f32),
            pltpu.VMEM((n, 2, 3) + turned, bf16),
            pltpu.VMEM((n, 2, 3) + turned, bf16),
            pltpu.VMEM((2,) + turned, bf16),
            pltpu.VMEM((2,) + turned, bf16),
            pltpu.VMEM((2, 2, 2) + tokens, f32),
            pltpu.VMEM((2, 2, 3) + tokens, bf16),
            pltpu.VMEM((2, 2, 3) + tokens, bf16),
            pltpu.VMEM(turned, f32),
            pltpu.SemaphoreType.DMA((N_SEM,)),
            pltpu.SemaphoreType.DMA((N_SEM,)),
        ],
        compiler_params=pltpu.CompilerParams(
            collective_id=0, has_side_effects=True, vmem_limit_bytes=60 * 1024 * 1024
        ),
        cost_estimate=pl.CostEstimate(
            flops=12 * n * ROWS * ROWS * HEAD_DIM, bytes_accessed=16 << 20, transcendentals=n * ROWS * ROWS
        ),
        name="attention",
    )(queries, key_input, values, cotangent, positions, lengths)
    return pl.pallas_call(
        hand_over,
        out_shape=[shape] * 4,
        in_specs=[hbm] * 4,
        out_specs=[hbm] * 4,
        scratch_shapes=[
            pltpu.VMEM((4, 1, TOK, HEADS_DEV * HEAD_DIM), bf16),
            pltpu.SemaphoreType.DMA((4,)),
            pltpu.SemaphoreType.DMA((4,)),
        ],
        name="hand_over",
    )(*results)


def solution(mesh):
    split = P("tower", "seq", "rep")
    return jax.shard_map(
        body,
        mesh=mesh,
        in_specs=(split, split, split, split, P("tower", "seq"), P("tower", "seq")),
        out_specs=(split, split, split, split),
        check_vma=False,
    )
```

```python
import math

import jax
import jax.numpy as jnp
from jax import lax
from jax.experimental import pallas as pl
from jax.experimental.pallas import tpu as pltpu
from jax.sharding import PartitionSpec as P

HEAD_DIM = 128
HEADS_DEV = 3
TOK = 384
ROWS = 4 * TOK
HALF = 2 * TOK
QCOLS = 12 * TOK
N_SEM = 80
SCALE = 1.0 / math.sqrt(HEAD_DIM)
SCALE_LOG2 = SCALE * math.log2(math.e)
MESH = pl.DeviceIdType.MESH
NN = (((1,), (0,)), ((), ()))
f32 = jnp.float32
bf16 = jnp.bfloat16


def dot(a, b):
    return lax.dot_general(a, b, NN, preferred_element_type=f32)


def rows(slot):
    return pl.ds(slot * TOK, TOK)


def kernel(
    q_hbm, k_hbm, v_hbm, g_hbm, pos_in, len_in,
    o_hbm, dq_hbm, dk_hbm, dv_hbm,
    ins, outs, in_sem, out_sem,
    khead, vhead, qhead, ghead,
    kbuf, vbuf, ktbuf, vtbuf, qt, gt, qr, gr, gts, lens,
    score, prob, dscore,
    stat_out, stat_in, oq_own, oq_send, oq_recv, oq_mate_send, oq_mate_recv,
    kv_own, kv_send, kv_recv, tables,
    send_sem, recv_sem,
):
    t, s, r = lax.axis_index("tower"), lax.axis_index("seq"), lax.axis_index("rep")
    x = s // 2
    odd = lax.rem(x, 2)
    mate = (t, s + 2 - 4 * odd, r)
    cross = (t, lax.rem(s + 6 + 4 * odd, 8), r)
    sibling = (t, s + 1 - 2 * lax.rem(s, 2), r)
    peer = (1 - t, s, r)
    mine = 2 * lax.rem((x + 1) // 2, 2)
    theirs = 2 - mine

    loads = {}
    for n, (name, src) in enumerate((("k", k_hbm), ("q", q_hbm), ("v", v_hbm), ("g", g_hbm))):
        loads[name] = pltpu.make_async_copy(src.at[0], ins.at[n], in_sem.at[n])
        loads[name].start()
    k_in, q_in, v_in, g_in = (ins.at[n] for n in range(4))
    stores = []

    def store(n, out, h, block):
        outs[n, :, head_cols(h)] = block
        copy = pltpu.make_async_copy(
            outs.at[n, :, head_cols(h)], out.at[0, :, head_cols(h)], out_sem.at[len(stores)]
        )
        copy.start()
        stores.append(copy)

    copies = {}

    def plan(name, src, dst, target):
        n = len(copies)
        copies[name] = pltpu.make_async_remote_copy(
            src_ref=src, dst_ref=dst, send_sem=send_sem.at[n], recv_sem=recv_sem.at[n],
            device_id=target, device_id_type=MESH,
        )

    def start(*names):
        for name in names:
            copies[name].start()

    def arrived(*names):
        for name in names:
            copies[name].wait_recv()

    for n in range(2):
        part = pl.ds(n * TOK // 2, TOK // 2)
        first, third = pl.ds(TOK + n * TOK // 2, TOK // 2), pl.ds(3 * TOK + n * TOK // 2, TOK // 2)
        for name, head, buf in (("k", khead, kbuf), ("v", vhead, vbuf)):
            plan((name + "_m", n), head.at[theirs, part], buf.at[0, first], mate)
            plan((name + "_f", n), buf.at[0, first], buf.at[0, third], cross)
    plan("q_m", qhead.at[theirs], qt.at[:, rows(4)], mate)
    plan("g_m", ghead.at[theirs], gt.at[:, rows(4)], mate)
    plan("k_c", khead.at[mine], kbuf.at[0, rows(2)], cross)
    plan("v_c", vhead.at[mine], vbuf.at[0, rows(2)], cross)
    plan("k1_m", khead.at[1], kbuf.at[1, rows(1)], mate)
    plan("v1_m", vhead.at[1], vbuf.at[1, rows(1)], mate)
    plan("k1_c", khead.at[1], kbuf.at[1, rows(2)], cross)
    plan("v1_c", vhead.at[1], vbuf.at[1, rows(2)], cross)
    plan("k1_f", kbuf.at[1, rows(1)], kbuf.at[1, rows(3)], cross)
    plan("v1_f", vbuf.at[1, rows(2)], vbuf.at[1, rows(3)], mate)
    plan("l_m", lens.at[0], lens.at[1], mate)
    plan("l_c", lens.at[0], lens.at[2], cross)
    plan("l_f", lens.at[1], lens.at[3], cross)
    for v in range(3):
        for name, buf in (("q", qt), ("g", gt)):
            plan((name + "_s", v), buf.at[:, rows(4 * v)], buf.at[:, rows(4 * v + 1)], sibling)
            plan((name + "_t", v), buf.at[:, rows(4 * v)], buf.at[:, rows(4 * v + 2)], peer)
            plan((name + "_f", v), buf.at[:, rows(4 * v + 2)], buf.at[:, rows(4 * v + 3)], sibling)
        for w in range(2):
            plan(("o_s1", v, w), oq_send.at[v, w, 0], oq_recv.at[v, w, 0], sibling)
            plan(("o_s3", v, w), oq_send.at[v, w, 1], oq_recv.at[v, w, 1], sibling)
            plan(("o_t", v, w), oq_send.at[v, w, 2], oq_recv.at[v, w, 2], peer)
    for half in range(6):
        plan(("st", half), stat_out.at[half], stat_in.at[half], sibling)
    for w in range(2):
        plan(("o_m", w), oq_mate_send.at[w], oq_mate_recv.at[w], mate)
        plan(("p2", w), kv_send.at[0, w, 0], kv_recv.at[0, w, 0], cross)
        plan(("p3", w), kv_send.at[0, w, 1], kv_recv.at[0, w, 1], cross)
        plan(("p1", w), kv_send.at[0, w, 2], kv_recv.at[0, w, 2], mate)
        plan(("s3", w), kv_send.at[1, w, 0], kv_recv.at[1, w, 0], (cross, mate)[w])
        plan(("s1", w), kv_send.at[1, w, 1], kv_recv.at[1, w, 1], mate)
        plan(("s2", w), kv_send.at[1, w, 2], kv_recv.at[1, w, 2], cross)

    barrier = pltpu.get_barrier_semaphore()
    for device in (mate, cross, sibling, peer):
        pl.semaphore_signal(barrier, inc=1, device_id=device, device_id_type=MESH)

    length = len_in[...]
    lens[0] = jnp.broadcast_to(length, (8, 128))
    exponent = lax.broadcasted_iota(jnp.int32, (64, TOK), 0).astype(f32)
    angles = jnp.exp(-math.log(10000.0) * exponent / 64) * pos_in[...].astype(f32)
    cos, sin = jnp.cos(angles), jnp.sin(angles)
    tables[0:64, :] = cos
    tables[64:128, :] = sin
    turned = jnp.transpose(tables[...])
    swapped = pltpu.roll(turned, 64, 1)
    low = lax.broadcasted_iota(jnp.int32, (TOK, HEAD_DIM), 1) < 64
    tables_rows = jnp.where(low, turned, swapped), jnp.where(low, -swapped, turned)
    present_rows = lax.broadcasted_iota(jnp.int32, (TOK, HEAD_DIM), 0) < length
    present_cols = lax.broadcasted_iota(jnp.int32, (1, TOK), 1) < length

    def prepare_keys(h):
        cos_rows, sin_rows = tables_rows
        key = k_in[:, h * HEAD_DIM : (h + 1) * HEAD_DIM].astype(f32)
        key = key * cos_rows + pltpu.roll(key, 64, 1) * sin_rows
        key = jnp.where(present_rows, key, key[0:1, :])
        khead[h] = key.astype(bf16)

    def prepare_queries(h):
        cols = slice(h * HEAD_DIM, (h + 1) * HEAD_DIM)
        query = jnp.transpose(q_in[:, cols].astype(f32))
        x1, x2 = query[0:64, :], query[64:128, :]
        qhead[h, 0:64, :] = (x1 * cos - x2 * sin).astype(bf16)
        qhead[h, 64:128, :] = (x2 * cos + x1 * sin).astype(bf16)
        grad = jnp.transpose(g_in[:, cols].astype(f32))
        ghead[h] = jnp.where(present_cols, grad, 0.0).astype(bf16)

    loads["k"].wait()
    prepare_keys(0)
    prepare_keys(2)
    pl.semaphore_wait(barrier, 4)
    start(("k_m", 0), ("k_m", 1), "k_c", "l_m", "l_c")
    kbuf[0, 0:TOK, :] = khead[mine]
    loads["q"].wait()
    loads["g"].wait()
    prepare_queries(0)
    prepare_queries(2)
    start("q_m")
    qt[:, 0:TOK] = qhead[mine]
    start(("q_s", 0), ("q_t", 0))
    loads["v"].wait()
    for h in range(HEADS_DEV):
        vhead[h] = v_in[:, h * HEAD_DIM : (h + 1) * HEAD_DIM]
    start(("v_m", 0), ("v_m", 1), "g_m")
    gt[:, 0:TOK] = ghead[mine]
    start(("g_s", 0), ("g_t", 0))
    vbuf[0, 0:TOK, :] = vhead[mine]

    def valid_row(slot):
        return (
            lax.broadcasted_iota(jnp.int32, (1, TOK), 1) < lens[slot][0:1, 0:1]
        ).astype(f32)

    def turn_keys(st, slot):
        valid = valid_row(slot)
        cols = rows(slot)
        ktbuf[st, :, cols] = (jnp.transpose(kbuf[st, cols, :].astype(f32)) * valid).astype(bf16)

    def turn_values(st, slot):
        valid = valid_row(slot)
        cols = rows(slot)
        vtbuf[st, 0:128, cols] = (jnp.transpose(vbuf[st, cols, :].astype(f32)) * valid).astype(bf16)
        vtbuf[st, 128:144, cols] = jnp.broadcast_to(valid, (16, TOK)).astype(bf16)

    def cols_of(half):
        return pl.ds(half * HALF, HALF)

    def prob_cols(half):
        return pl.ds((half % 4) * HALF, HALF)

    def scores(st, half, before=None):
        query = qt[:, cols_of(half)]
        top = None
        for slot in range(4):
            if before is not None:
                before(slot)
            part = dot(kbuf[st, rows(slot), :], query)
            score[half % 2, rows(slot), :] = part
            part = jnp.max(part.reshape(TOK // 8, 8, HALF), axis=0)
            top = part if top is None else jnp.maximum(top, part)
        top = jnp.max(top, axis=0, keepdims=True) * SCALE_LOG2
        stat_out[half, 0:1, :] = top
        for slot in range(4):
            prob[rows(slot), prob_cols(half)] = jnp.exp2(
                score[half % 2, rows(slot), :] * SCALE_LOG2 - top
            ).astype(bf16)

    def outputs(st, half):
        cols = cols_of(half)
        out = dot(vtbuf[st], prob[:, prob_cols(half)])
        oq_own[0, :, cols] = out[0:128, :]
        stat_out[half, 1:2, :] = out[128:129, :]

    def send_stats(half):
        cols = cols_of(half)
        stat_out[half, 2:3, :] = jnp.sum(
            oq_own[0, :, cols] * gt[:, cols].astype(f32), axis=0, keepdims=True
        )
        start(("st", half))

    def turn_queries(half):
        qr[cols_of(half), :] = jnp.transpose(qt[:, cols_of(half)].astype(f32)).astype(bf16)

    def normalise(half):
        arrived(("st", half))
        mine_, other = stat_out[half], stat_in[half]
        other = jnp.concatenate([other[:, TOK:], other[:, 0:TOK]], axis=1)
        top = jnp.maximum(mine_[0:1], other[0:1])
        grow, grow_other = jnp.exp2(mine_[0:1] - top), jnp.exp2(other[0:1] - top)
        inverse = 1.0 / (mine_[1:2] * grow + other[1:2] * grow_other)
        factor, factor_other = grow * inverse, grow_other * inverse
        row_dot = (factor * mine_[2:3] + factor_other * other[2:3]) * factor
        cols = cols_of(half)
        scaled = gt[:, cols].astype(f32) * factor
        gts[:, cols] = scaled.astype(bf16)
        gr[cols, :] = jnp.transpose(scaled).astype(bf16)
        oq_own[0, :, cols] = oq_own[0, :, cols] * factor
        return row_dot

    def share(v, w):
        oq_send[v, w, 0] = oq_own[w, :, rows(4 * v + 1)].astype(bf16)
        oq_send[v, w, 1] = oq_own[w, :, rows(4 * v + 3)].astype(bf16)
        start(("o_s3", v, w), ("o_s1", v, w))

    def pass_on(v, w):
        arrived(("o_s3", v, w))
        both = oq_own[w, :, rows(4 * v + 2)] + oq_recv[v, w, 1].astype(f32)
        oq_send[v, w, 2] = both.astype(bf16)
        start(("o_t", v, w))

    def total_queries(v, w):
        arrived(("o_s1", v, w), ("o_t", v, w))
        total = oq_own[w, :, rows(4 * v)] + oq_recv[v, w, 0].astype(f32)
        return (total + oq_recv[v, w, 2].astype(f32)).astype(bf16)

    def head_cols(h):
        if isinstance(h, int):
            return pl.ds(h * HEAD_DIM, HEAD_DIM)
        return pl.ds(pl.multiple_of(h * HEAD_DIM, HEAD_DIM), HEAD_DIM)

    def write_queries(h, w, total):
        total = total.astype(f32)
        if w == 0:
            total = jnp.where(present_cols, total, 0.0)
            store(0, o_hbm, h, jnp.transpose(total).astype(bf16))
        else:
            cos, sin = tables[0:64, :], tables[64:128, :]
            d1, d2 = total[0:64, :], total[64:128, :]
            total = jnp.concatenate([d1 * cos + d2 * sin, d2 * cos - d1 * sin], axis=0)
            store(1, dq_hbm, h, jnp.transpose(total).astype(bf16))

    def write_keys(h, w, total):
        total = jnp.where(present_rows, total.astype(f32), 0.0)
        if w == 0:
            cos_rows, sin_rows = tables_rows
            total = total.astype(bf16).astype(f32)
            total = total * cos_rows - pltpu.roll(total, 64, 1) * sin_rows
            store(2, dk_hbm, h, total.astype(bf16))
        else:
            store(3, dv_hbm, h, total.astype(bf16))

    def score_gradients(st, keys, half, row_dot):
        grad = dot(vbuf[st, keys, :], gts[:, cols_of(half)])
        grad = prob[keys, prob_cols(half)].astype(f32) * (grad - row_dot)
        dscore[keys, prob_cols(half)] = grad.astype(bf16)

    def key_gradients(st, keys, halves):
        width = pl.ds(0, len(halves) * HALF)
        queries = pl.ds(halves[0] * HALF, len(halves) * HALF)
        dk = dot(dscore[keys, width], qr[queries, :]) * SCALE
        dv = dot(prob[keys, width], gr[queries, :])
        return dk, dv

    def query_gradients(st, half):
        oq_own[1, :, cols_of(half)] = dot(ktbuf[st], dscore[:, prob_cols(half)]) * SCALE

    def relay(got, *onward):
        arrived(got)
        start(*onward)

    def before(slot):
        if slot == 2:
            relay(("q_t", 0), ("q_f", 0))
            arrived("k_c")
        if slot == 3:
            relay("q_m", ("q_s", 1), ("q_t", 1))
            arrived(("k_f", 0), ("k_f", 1))

    relay(("k_m", 0), ("k_f", 0))
    relay(("k_m", 1), ("k_f", 1), "v_c")
    arrived(("q_s", 0))
    scores(0, 0, before)
    relay(("v_m", 0), ("v_f", 0))
    relay(("v_m", 1), ("v_f", 1))
    relay("l_m", "l_f")
    prepare_keys(1)
    kbuf[1, 0:TOK, :] = khead[1]
    vbuf[1, 0:TOK, :] = vhead[1]
    start("k1_m", "k1_c", "v1_m", "v1_c")
    arrived(("q_f", 0))
    scores(0, 1)
    relay(("g_t", 0), ("g_f", 0))
    arrived(("q_s", 1))
    scores(0, 2)
    relay(("q_t", 1), ("q_f", 1))
    relay("g_m", ("g_s", 1), ("g_t", 1))
    prepare_queries(1)
    qt[:, 8 * TOK : 9 * TOK] = qhead[1]
    gt[:, 8 * TOK : 9 * TOK] = ghead[1]
    start(("q_s", 2), ("q_t", 2), ("g_s", 2), ("g_t", 2))
    arrived("v_c", "l_c", "l_f", ("v_f", 0), ("v_f", 1))
    for slot in range(4):
        turn_values(0, slot)
    outputs(0, 0)
    outputs(0, 1)
    arrived(("g_s", 0), ("g_f", 0))
    send_stats(0)
    send_stats(1)
    arrived(("q_f", 1))
    scores(0, 3)
    for slot in range(4):
        turn_keys(0, slot)
    for half in range(4):
        turn_queries(half)
    outputs(0, 2)
    outputs(0, 3)

    near, far = pl.ds(0, HALF), pl.ds(HALF, HALF)
    row_dots = [None] * 6
    for half in (0, 1):
        row_dots[half] = normalise(half)
    share(0, 0)
    for half in (0, 1):
        score_gradients(0, far, half, row_dots[half])
    relay(("g_t", 1), ("g_f", 1))
    arrived(("g_s", 1))
    send_stats(2)
    for half in (0, 1):
        score_gradients(0, near, half, row_dots[half])
    arrived(("g_f", 1))
    send_stats(3)
    pass_on(0, 0)
    for half in (0, 1):
        query_gradients(0, half)
    share(0, 1)
    relay("k1_m", "k1_f")
    relay("v1_c", "v1_f")
    for half in (2, 3):
        row_dots[half] = normalise(half)
    share(1, 0)
    for half in (2, 3):
        score_gradients(0, far, half, row_dots[half])
    totals = key_gradients(0, far, (0, 1, 2, 3))
    for w in range(2):
        kv_send[0, w, 1] = totals[w][TOK:].astype(bf16)
        start(("p3", w))
    for w in range(2):
        kv_send[0, w, 0] = totals[w][0:TOK].astype(bf16)
        start(("p2", w))
    pass_on(1, 0)
    relay(("q_t", 2), ("q_f", 2))
    relay(("g_t", 2), ("g_f", 2))
    for half in (2, 3):
        score_gradients(0, near, half, row_dots[half])
    for half in (2, 3):
        query_gradients(0, half)
    share(1, 1)
    pass_on(0, 1)
    totals = key_gradients(0, near, (0, 1, 2, 3))
    pass_on(1, 1)
    for w, total in enumerate(totals):
        kv_own[0, w, 0] = total[0:TOK]
        kv_own[0, w, 1] = total[TOK:]

    arrived("k1_c", "k1_f", ("q_s", 2), ("q_f", 2))
    scores(1, 4)
    for w in range(2):
        arrived(("p3", w))
        kv_send[0, w, 2] = (kv_own[0, w, 1] + kv_recv[0, w, 1].astype(f32)).astype(bf16)
        start(("p1", w))
    scores(1, 5)
    oq_mate_send[0] = total_queries(1, 0)
    start(("o_m", 0))
    arrived("v1_m", "v1_f", ("g_s", 2), ("g_f", 2))
    for slot in range(4):
        turn_values(1, slot)
    outputs(1, 4)
    send_stats(4)
    outputs(1, 5)
    send_stats(5)
    for slot in range(4):
        turn_keys(1, slot)
    turn_queries(4)
    turn_queries(5)
    for w in range(2):
        arrived(("p2", w))
        write_keys(mine, w, (kv_own[0, w, 0] + kv_recv[0, w, 0].astype(f32)).astype(bf16))
    write_queries(mine, 0, total_queries(0, 0))

    for half in (4, 5):
        row_dots[half] = normalise(half)
    share(2, 0)

    def gradients(slot):
        for half in (4, 5):
            score_gradients(1, rows(slot), half, row_dots[half])

    def gather_gradients(slot):
        return key_gradients(1, rows(slot), (4, 5))

    gradients(3)
    dk, dv = gather_gradients(3)
    kv_send[1, 0, 0] = dk.astype(bf16)
    start(("s3", 0))
    kv_send[1, 1, 0] = dv.astype(bf16)
    start(("s3", 1))
    gradients(2)
    dk, dv = gather_gradients(2)
    kv_send[1, 0, 2] = dk.astype(bf16)
    start(("s2", 0))
    kv_own[1, 1, 1] = dv
    pass_on(2, 0)
    oq_mate_send[1] = total_queries(1, 1)
    start(("o_m", 1))
    gradients(1)
    gradients(0)
    for half in (4, 5):
        query_gradients(1, half)
    share(2, 1)
    dk, dv = gather_gradients(1)
    kv_send[1, 1, 1] = dv.astype(bf16)
    start(("s1", 1))
    arrived(("s3", 0))
    kv_send[1, 0, 1] = (dk + kv_recv[1, 0, 0].astype(f32)).astype(bf16)
    start(("s1", 0))
    arrived(("s3", 1))
    kv_send[1, 1, 2] = (kv_own[1, 1, 1] + kv_recv[1, 1, 0].astype(f32)).astype(bf16)
    start(("s2", 1))
    dk, dv = gather_gradients(0)
    pass_on(2, 1)
    kv_own[1, 0, 0] = dk
    kv_own[1, 1, 0] = dv

    write_queries(mine, 1, total_queries(0, 1))
    for w in range(2):
        arrived(("p1", w))
        write_keys(theirs, w, kv_recv[0, w, 2])
    for w in range(2):
        arrived(("o_m", w))
        write_queries(theirs, w, oq_mate_recv[w])
    write_queries(1, 0, total_queries(2, 0))
    for w in (1, 0):
        arrived(("s1", w), ("s2", w))
        total = kv_own[1, w, 0] + kv_recv[1, w, 1].astype(f32) + kv_recv[1, w, 2].astype(f32)
        write_keys(1, w, total.astype(bf16))
    write_queries(1, 1, total_queries(2, 1))
    for copy in stores:
        copy.wait()
    for copy in copies.values():
        copy.wait_send()


def hand_over(*refs):
    sources, results, (held, load_sem, store_sem) = refs[:4], refs[4:8], refs[8:]
    loads = [pltpu.make_async_copy(sources[n], held.at[n], load_sem.at[n]) for n in range(4)]
    stores = [pltpu.make_async_copy(held.at[n], results[n], store_sem.at[n]) for n in range(4)]
    for copy in loads:
        copy.start()
    for load, copy in zip(loads, stores):
        load.wait()
        copy.start()
    for copy in stores:
        copy.wait()


def body(queries, key_input, values, cotangent, positions, lengths):
    shape = jax.ShapeDtypeStruct(queries.shape, bf16)
    vmem = pl.BlockSpec(memory_space=pltpu.VMEM)
    hbm = pl.BlockSpec(memory_space=pl.ANY)
    tokens, turned = (TOK, HEAD_DIM), (HEAD_DIM, TOK)
    n = HEADS_DEV
    results = pl.pallas_call(
        kernel,
        out_shape=[shape] * 4,
        in_specs=[hbm] * 4 + [vmem] * 2,
        out_specs=[hbm] * 4,
        scratch_shapes=[
            pltpu.VMEM((4, TOK, HEADS_DEV * HEAD_DIM), bf16),
            pltpu.VMEM((4, TOK, HEADS_DEV * HEAD_DIM), bf16),
            pltpu.SemaphoreType.DMA((4,)),
            pltpu.SemaphoreType.DMA((12,)),
            pltpu.VMEM((n,) + tokens, bf16),
            pltpu.VMEM((n,) + tokens, bf16),
            pltpu.VMEM((n,) + turned, bf16),
            pltpu.VMEM((n,) + turned, bf16),
            pltpu.VMEM((2, ROWS, HEAD_DIM), bf16),
            pltpu.VMEM((2, ROWS, HEAD_DIM), bf16),
            pltpu.VMEM((2, HEAD_DIM, ROWS), bf16),
            pltpu.VMEM((2, HEAD_DIM + 16, ROWS), bf16),
            pltpu.VMEM((HEAD_DIM, QCOLS), bf16),
            pltpu.VMEM((HEAD_DIM, QCOLS), bf16),
            pltpu.VMEM((QCOLS, HEAD_DIM), bf16),
            pltpu.VMEM((QCOLS, HEAD_DIM), bf16),
            pltpu.VMEM((HEAD_DIM, QCOLS), bf16),
            pltpu.VMEM((4, 8, 128), jnp.int32),
            pltpu.VMEM((2, ROWS, HALF), f32),
            pltpu.VMEM((ROWS, 4 * HALF), bf16),
            pltpu.VMEM((ROWS, 4 * HALF), bf16),
            pltpu.VMEM((6, 8, HALF), f32),
            pltpu.VMEM((6, 8, HALF), f32),
            pltpu.VMEM((2, HEAD_DIM, QCOLS), f32),
            pltpu.VMEM((n, 2, 3) + turned, bf16),
            pltpu.VMEM((n, 2, 3) + turned, bf16),
            pltpu.VMEM((2,) + turned, bf16),
            pltpu.VMEM((2,) + turned, bf16),
            pltpu.VMEM((2, 2, 2) + tokens, f32),
            pltpu.VMEM((2, 2, 3) + tokens, bf16),
            pltpu.VMEM((2, 2, 3) + tokens, bf16),
            pltpu.VMEM(turned, f32),
            pltpu.SemaphoreType.DMA((N_SEM,)),
            pltpu.SemaphoreType.DMA((N_SEM,)),
        ],
        compiler_params=pltpu.CompilerParams(
            collective_id=0, has_side_effects=True, vmem_limit_bytes=60 * 1024 * 1024
        ),
        cost_estimate=pl.CostEstimate(
            flops=12 * n * ROWS * ROWS * HEAD_DIM, bytes_accessed=16 << 20, transcendentals=n * ROWS * ROWS
        ),
        name="attention",
    )(queries, key_input, values, cotangent, positions, lengths)
    return pl.pallas_call(
        hand_over,
        out_shape=[shape] * 4,
        in_specs=[hbm] * 4,
        out_specs=[hbm] * 4,
        scratch_shapes=[
            pltpu.VMEM((4, 1, TOK, HEADS_DEV * HEAD_DIM), bf16),
            pltpu.SemaphoreType.DMA((4,)),
            pltpu.SemaphoreType.DMA((4,)),
        ],
        name="hand_over",
    )(*results)


def solution(mesh):
    split = P("tower", "seq", "rep")
    return jax.shard_map(
        body,
        mesh=mesh,
        in_specs=(split, split, split, split, P("tower", "seq"), P("tower", "seq")),
        out_specs=(split, split, split, split),
        check_vma=False,
    )
```
